32 devices in a mesh: ctx: 16 (over z, x, core), tp: 2 (over y).
Axes of the slice: x: 2, y: 2, z: 4, core: 2. Of those that a mesh axis runs over, the one named last changes fastest.
Arguments:
- ctx_queries: bfloat16 [4096, 4096], P('ctx', 'tp'), may hold values from -5 to 5
- ctx_keys: bfloat16 [4096, 1024], P('ctx', 'tp'), may hold values from -5 to 5
- ctx_values: bfloat16 [4096, 1024], P('ctx', 'tp'), may hold values from -18 to 18
- query_queries: bfloat16 [512, 4096], P(None, 'tp'), may hold values from -5 to 5
- query_keys: bfloat16 [512, 1024], P('ctx', 'tp'), may hold values from -5 to 5
- query_values: bfloat16 [512, 1024], P('ctx', 'tp'), may hold values from -18 to 18
- out_weight: bfloat16 [4096, 4096], P('tp', 'ctx'), may hold values from -0.09375 to 0.09375
Outputs:
- ctx_out: bfloat16 [4096, 4096], P('ctx', 'tp')
- query_out: bfloat16 [512, 4096], P('tp', 'ctx')
The draws below stay inside these ranges and needn't reach their ends.
All inputs are finite; a program needn't handle non-finite values.
Results may differ from the reference program's by a relative error of at most 0.0049.
Values may be sent and summed in bfloat16 or wider, within the bound.
A program may use at most 192 MiB of HBM per device.

```python
import jax
import jax.numpy as jnp
from jax import lax

D = 4096
HEADS = 32
KV_HEADS = 8
HD = 128
BLK = 256
QL = 512
CONTEXT = 4096
N_CTX = 16


def base_field(key, rows, cols):
    return jnp.clip(1.565 * jax.random.normal(key, (rows, cols), jnp.float32), -5.0, 5.0)


def draw_ctx_keys(key, part):
    field = base_field(jax.random.fold_in(key, 11), CONTEXT, KV_HEADS * HD)
    return field.astype(jnp.bfloat16)


def draw_ctx_queries(key, part):
    field = base_field(jax.random.fold_in(key, 23), CONTEXT, HEADS * HD)
    return field.astype(jnp.bfloat16)


def draw_query_queries(key, part):
    field = base_field(jax.random.fold_in(key, 37), QL, HEADS * HD)
    return field.astype(jnp.bfloat16)


def block_levels(own_key, extent, cuts, low, top_value):
    gain, own = 1.0, jax.random.fold_in(own_key, 6)
    for dim, blocks in cuts:
        steps = jnp.exp(jax.random.uniform(jax.random.fold_in(own, dim), (blocks,), jnp.float32, low / len(cuts), top_value / len(cuts)))
        gain = gain * jnp.repeat(steps, extent[dim] // blocks).reshape([-1 if axis == dim else 1 for axis in range(len(extent))])
    return gain


def gaussian(key, dims, width, limit, split=(), kind=jnp.bfloat16):
    factor_of = block_levels(key, dims, split, -0.22, 0.18) if split else 1.0
    drawn = jax.random.normal(key, dims, jnp.float32) * width * factor_of
    return jnp.minimum(jnp.maximum(drawn, -limit), limit).astype(kind)


def setup_inputs(seed: int = 0) -> dict:
    splits = jax.random.split(jax.random.key(seed), 8)
    return {
        "ctx_queries": draw_ctx_queries(jax.random.fold_in(splits[7], 71), 0),
        "ctx_keys": draw_ctx_keys(jax.random.fold_in(splits[7], 71), 0),
        "ctx_values": gaussian(splits[2], (CONTEXT, KV_HEADS * HD), 3.0, 18.0, ((0, 16), (1, 2))),
        "query_queries": draw_query_queries(jax.random.fold_in(splits[7], 71), 0),
        "query_keys": gaussian(splits[4], (QL, KV_HEADS * HD), 1.565, 5.0, ((0, 16), (1, 2))),
        "query_values": gaussian(splits[5], (QL, KV_HEADS * HD), 3.0, 18.0, ((0, 16), (1, 2))),
        "out_weight": gaussian(splits[6], (HEADS * HD, D), (HEADS * HD) ** -0.5, 0.09375, ((0, 2), (1, 16))),
    }


def attend_part(query_part, key_part, value_part, visible):
    scale = HD ** -0.5
    scores = jnp.einsum('tkgd,skd->tkgs', query_part.astype(jnp.float32), key_part.astype(jnp.float32)) * scale
    scores = jnp.where(visible[:, None, None, :], scores, -jnp.inf)
    top = jnp.max(scores, axis=-1)
    weights = jnp.exp(scores - top[..., None])
    total = jnp.sum(weights, axis=-1)
    probs = weights.astype(jnp.bfloat16)
    summed = jnp.einsum('tkgs,skd->tkgd', probs.astype(jnp.float32), value_part.astype(jnp.float32))
    return top, total, summed


def combine_parts(first, second):
    top = jnp.maximum(first[0], second[0])
    left = jnp.exp(first[0] - top)
    right = jnp.exp(second[0] - top)
    total = first[1] * left + second[1] * right
    summed = first[2] * left[..., None] + second[2] * right[..., None]
    return top, total, summed


def reference(ctx_queries, ctx_keys, ctx_values, query_queries, query_keys, query_values, out_weight):
    group = HEADS // KV_HEADS
    share = QL // N_CTX
    ctx_grid = ctx_queries.reshape(N_CTX, BLK, KV_HEADS, group, HD)
    key_grid = ctx_keys.reshape(N_CTX, BLK, KV_HEADS, HD)
    value_grid = ctx_values.reshape(N_CTX, BLK, KV_HEADS, HD)
    query_grid = query_queries.reshape(QL, KV_HEADS, group, HD)
    qkey_grid = query_keys.reshape(N_CTX, share, KV_HEADS, HD)
    qvalue_grid = query_values.reshape(N_CTX, share, KV_HEADS, HD)
    position = jnp.arange(BLK)
    causal = position[:, None] >= position[None, :]

    def context_block(block):
        key_rows = jnp.concatenate([key_grid[0], key_grid[block]], 0)
        value_rows = jnp.concatenate([value_grid[0], value_grid[block]], 0)
        anchor_seen = jnp.broadcast_to(block > 0, (BLK, BLK))
        visible = jnp.concatenate([anchor_seen, causal], 1)
        top, total, summed = attend_part(ctx_grid[block], key_rows, value_rows, visible)
        return (summed / total[..., None]).astype(jnp.bfloat16).reshape(BLK, HEADS * HD)

    ctx_out = lax.map(context_block, jnp.arange(N_CTX)).reshape(N_CTX * BLK, HEADS * HD)

    query_pos = jnp.arange(QL)

    def fold_block(carry, block):
        key_rows = jnp.concatenate([key_grid[block], qkey_grid[block]], 0)
        value_rows = jnp.concatenate([value_grid[block], qvalue_grid[block]], 0)
        key_pos = block * share + jnp.arange(share)
        visible = jnp.concatenate([jnp.ones((QL, BLK), dtype=bool), query_pos[:, None] >= key_pos[None, :]], 1)
        part = attend_part(query_grid, key_rows, value_rows, visible)
        return combine_parts(carry, part), None

    start = (jnp.full((QL, KV_HEADS, group), -jnp.inf, jnp.float32),
             jnp.zeros((QL, KV_HEADS, group), jnp.float32),
             jnp.zeros((QL, KV_HEADS, group, HD), jnp.float32))
    final, unused = lax.scan(fold_block, start, jnp.arange(N_CTX))
    attended = (final[2] / final[1][..., None]).astype(jnp.bfloat16).reshape(QL, HEADS * HD)
    query_out = jnp.dot(attended, out_weight, preferred_element_type=jnp.float32).astype(jnp.bfloat16)
    return ctx_out, query_out
```

```python
import functools
import math

import jax
import jax.numpy as jnp
from jax import lax
from jax.experimental import pallas as pl
from jax.experimental.pallas import tpu as pltpu
from jax.sharding import PartitionSpec as P

HD = 128
MESH = pl.DeviceIdType.MESH
COEF = HD ** (-0.5) * math.log2(math.e)
F32 = jnp.float32
BF16 = jnp.bfloat16
NEG = float("-inf")


def kernel(dims, cq_h, ck_h, cv_h, qq_h, qk_h, qv_h, w_h, co_h, qo_h, cq, ck, cv, ak, av, qq, w, kb, vb, kqb, vqb,
           acc, top, osend, lsend, orecv, lrecv, att, ysend, yrecv, co, qo, loc_sem, kv_s, kv_r, an_s, an_r, an_u,
           an_rs, an_rr, rs_s, rs_r, ag_r, ag_u, ag_d, ag_rs, ag_cs, y_s, y_r):
    groups, members, tps, kv_local, group, block, share, query_len = dims
    flat = group * query_len
    chunk = flat // members
    tile = min(256, chunk)
    pieces = math.gcd(members, block // 16)
    piece = block // pieces
    me = lax.axis_index("ctx")
    my_tp = lax.axis_index("tp")
    g = lax.div(me, members)
    m = lax.rem(me, members)
    pair = m + 1 - 2 * lax.rem(m, 2)

    def lanes(index):
        return pl.ds(pl.multiple_of(index * HD, HD), HD)

    def local(src, dst, i):
        return pltpu.make_async_copy(src, dst, loc_sem.at[i])

    def remote(src, dst, send, recv, to, axis="ctx"):
        return pltpu.make_async_remote_copy(src_ref=src, dst_ref=dst, send_sem=send, recv_sem=recv,
                                            device_id={axis: to}, device_id_type=MESH)

    wide = pl.ds(pl.multiple_of(g * (group * HD), HD), group * HD)
    own_rows = pl.ds(pl.multiple_of(g * share, share), share)
    loads = [
        local(qq_h.at[:, wide], qq, 0),
        local(ck_h.at[:, lanes(g)], kb.at[g], 1),
        local(cv_h.at[:, lanes(g)], vb.at[g], 2),
        local(ck_h, ck, 3),
        local(cv_h, cv, 4),
        local(cq_h, cq, 5),
        local(w_h, w, 6),
        local(qk_h.at[:, lanes(g)], kqb.at[own_rows], 7),
        local(qv_h.at[:, lanes(g)], vqb.at[own_rows], 8),
    ]
    if kqb.shape[0] > groups * share:
        kqb[...] = jnp.zeros_like(kqb)
        vqb[...] = jnp.zeros_like(vqb)
    for load in loads:
        load.start()

    @pl.when(me == 0)
    def _():
        local(ck_h, ak, 9).start()
        local(cv_h, av, 10).start()

    barrier = pltpu.get_barrier_semaphore()

    def greet_group(i, carry):
        to = g * members + lax.rem(m + i, members)
        pl.semaphore_signal(barrier, inc=1, device_id={"ctx": to}, device_id_type=MESH)
        return carry

    lax.fori_loop(1, members, greet_group, 0)
    for d in range(1, groups):
        to = lax.rem(g + d, groups) * members + m
        pl.semaphore_signal(barrier, inc=1, device_id={"ctx": to}, device_id_type=MESH)
    for d in range(1, tps):
        pl.semaphore_signal(barrier, inc=1, device_id={"tp": lax.rem(my_tp + d, tps)}, device_id_type=MESH)
    pl.semaphore_wait(barrier, members - 1 + groups - 1 + tps - 1)

    def piece_rows(p):
        return pl.ds(pl.multiple_of(p * piece, piece), piece)

    @pl.when(me == 0)
    def _():
        local(ck_h, ak, 9).wait()
        local(cv_h, av, 10).wait()
        for p in range(1, pieces):
            for k, buf in enumerate((ak, av)):
                remote(buf.at[piece_rows(p)], buf.at[piece_rows(p)], an_s.at[p, k], an_r.at[k], p).start()

    def kv_copies(to_group, slot):
        to = to_group * members + m
        rows = pl.ds(pl.multiple_of(slot * share, share), share)
        return [
            remote(ck_h.at[:, lanes(to_group)], kb.at[slot], kv_s.at[to_group, 0], kv_r.at[slot, 0], to),
            remote(cv_h.at[:, lanes(to_group)], vb.at[slot], kv_s.at[to_group, 1], kv_r.at[slot, 1], to),
            remote(qk_h.at[:, lanes(to_group)], kqb.at[rows], kv_s.at[to_group, 2], kv_r.at[slot, 2], to),
            remote(qv_h.at[:, lanes(to_group)], vqb.at[rows], kv_s.at[to_group, 3], kv_r.at[slot, 3], to),
        ]

    for d in range(1, groups):
        for copy in kv_copies(lax.rem(g + d, groups), g):
            copy.start()

    def attend(first_row, first, slot, with_query):
        head = lax.div(first_row, query_len)
        row = lax.rem(first_row, query_len)
        q = qq[pl.ds(pl.multiple_of(row, tile), tile), lanes(head)]
        keys, values = kb[slot], vb[slot]
        if with_query:
            keys = jnp.concatenate([keys, kqb[...]], 0)
            values = jnp.concatenate([values, vqb[...]], 0)
        values = jnp.concatenate([values, jnp.ones_like(values)], 1)
        s = lax.dot_general(q, keys, (((1,), (1,)), ((), ())), preferred_element_type=F32) * COEF
        if with_query:
            col = lax.broadcasted_iota(jnp.int32, s.shape, 1) - block
            at = lax.broadcasted_iota(jnp.int32, s.shape, 0) + row
            source = lax.div(jnp.maximum(col, 0), share)
            position = (source * members + m) * share + lax.rem(jnp.maximum(col, 0), share)
            seen = (col < 0) | ((at >= position) & (col < groups * share))
            s = jnp.where(seen, s, NEG)
        rows = pl.ds(pl.multiple_of(first_row, tile), tile)
        high = jnp.max(s, axis=1, keepdims=True)
        if not first:
            before = top[rows, :]
            high = jnp.maximum(high, before[:, :1])
        p = jnp.exp2(s - high).astype(BF16)
        o = jnp.dot(p, values, preferred_element_type=F32)
        if not first:
            o = o + acc[rows, :] * jnp.exp2(before[:, :1] - high)
        acc[rows, :] = o
        top[rows, :] = jnp.broadcast_to(high, (tile, HD))

    def sweep(slot, first):
        def step(t, carry):
            attend(t * tile, first, slot, False)
            return carry

        lax.fori_loop(0, flat // tile, step, 0, unroll=2)

    for i in (0, 1, 2):
        loads[i].wait()
    if groups > 1:
        sweep(g, True)

    for i in (3, 4, 5, 6, 7, 8):
        loads[i].wait()
    not_root = me > 0
    has_piece = m < pieces

    @pl.when(has_piece)
    def _():
        mine = piece_rows(m)
        for k, buf in enumerate((ak, av)):
            @pl.when(not_root)
            def _():
                remote(buf.at[mine], buf.at[mine], an_u.at[k], an_r.at[k], me).wait_recv()

            @pl.when(g + 1 < groups)
            def _():
                remote(buf.at[mine], buf.at[mine], an_u.at[k], an_r.at[k], lax.rem(me + members, groups * members)).start()

        def spread(i, carry):
            other = lax.rem(m + i, members)

            @pl.when((g > 0) | (other > 0))
            def _():
                for k, buf in enumerate((ak, av)):
                    remote(buf.at[mine], buf.at[mine], an_rs.at[other, k], an_rr.at[m, k], g * members + other).start()
            return carry

        lax.fori_loop(1, members, spread, 0)

    @pl.when(not_root)
    def _():
        def gather(p, carry):
            @pl.when(p != m)
            def _():
                for k, buf in enumerate((ak, av)):
                    remote(buf.at[piece_rows(p)], buf.at[piece_rows(p)], an_u.at[k], an_rr.at[p, k], me).wait_recv()
            return carry

        lax.fori_loop(0, pieces, gather, 0)

    def context_head(h):
        kv = lanes(lax.div(h, group))
        q = cq[:, lanes(h)]
        keys = jnp.concatenate([ak[:, kv], ck[:, kv]], 0)
        values = jnp.concatenate([av[:, kv], cv[:, kv]], 0)
        values = jnp.concatenate([values, jnp.ones_like(values)], 1)
        s = lax.dot_general(q, keys, (((1,), (1,)), ((), ())), preferred_element_type=F32) * COEF
        col = lax.broadcasted_iota(jnp.int32, s.shape, 1) - block
        at = lax.broadcasted_iota(jnp.int32, s.shape, 0)
        s = jnp.where((col <= at) & ((col >= 0) | not_root), s, NEG)
        p = jnp.exp2(s - jnp.max(s, axis=1, keepdims=True)).astype(BF16)
        o = jnp.dot(p, values, preferred_element_type=F32)
        co[:, lanes(h)] = (o[:, :HD] / o[:, HD:]).astype(BF16)

    def context_step(h, carry):
        context_head(h)
        return carry

    lax.fori_loop(0, kv_local * group, context_step, 0, unroll=2)
    store_ctx = local(co, co_h, 11)
    store_ctx.start()

    for d in range(1, groups):
        slot = lax.rem(g + d, groups)
        for copy in kv_copies(slot, slot):
            copy.wait_recv()
        if d < groups - 1:
            sweep(slot, False)
    last = lax.rem(g + groups - 1, groups)

    def part(to):
        rows = pl.ds(pl.multiple_of(to * chunk, chunk), chunk)
        total = acc[rows, HD:]
        return acc[rows, :HD] / total, top[rows, :] + jnp.log2(total)

    def attend_chunk(to):
        for t in range(chunk // tile):
            attend(to * chunk + t * tile, groups == 1, last, True)

    def part_copies(to, slot):
        target = g * members + to
        return [
            remote(osend.at[to], orecv.at[slot], rs_s.at[to, 0], rs_r.at[slot, 0], target),
            remote(lsend.at[to], lrecv.at[slot], rs_s.at[to, 1], rs_r.at[slot, 1], target),
        ]

    def send_part(i, carry):
        to = lax.rem(m + i, members)
        attend_chunk(to)
        out, lse = part(to)
        osend[to] = out.astype(BF16)
        lsend[to] = jnp.transpose(lse)[:8, :]
        for copy in part_copies(to, m):
            copy.start()
        return carry

    lax.fori_loop(1, members, send_part, 0)
    attend_chunk(m)
    own, own_lse = part(m)

    def wait_part(i, carry):
        for copy in part_copies(lax.rem(m + i, members), lax.rem(m + i, members)):
            copy.wait_recv()
        return carry

    lax.fori_loop(1, members, wait_part, 0)

    def lse_of(i):
        row = lrecv[lax.rem(m + i, members)][:1, :]
        return jnp.transpose(jnp.broadcast_to(row, (HD, chunk)))

    highest = lax.fori_loop(1, members, lambda i, high: jnp.maximum(high, lse_of(i)), own_lse)
    own_weight = jnp.exp2(own_lse - highest)

    def combine(i, carry):
        total, summed = carry
        weight = jnp.exp2(lse_of(i) - highest)
        return total + weight, summed + weight * orecv[lax.rem(m + i, members)].astype(F32)

    total, summed = lax.fori_loop(1, members, combine, (own_weight, own_weight * own))

    def place(of_group, of_member):
        start = of_member * chunk
        row = pl.multiple_of(lax.rem(start, query_len), chunk)
        return att.at[pl.ds(row, chunk), lanes(of_group * group + lax.div(start, query_len))]

    place(g, m)[...] = (summed / total).astype(BF16)

    def gathered(of_group, of_member, send, to):
        where = place(of_group, of_member)
        return remote(where, where, send, ag_r.at[of_group, of_member], to)

    def to_pair(of_group, of_member):
        return gathered(of_group, of_member, ag_cs.at[of_group, of_member], g * members + pair)

    def have(of_group):
        def across(i, carry):
            other = lax.rem(m + 2 * i, members)
            gathered(of_group, m, ag_rs.at[of_group, other], g * members + other).start()
            return carry

        lax.fori_loop(1, members // 2, across, 0)
        to_pair(of_group, m).start()

    def forward(of_group):
        def step(i, carry):
            other = lax.rem(m + 2 * i, members)
            gathered(of_group, other, ag_cs.at[of_group, other], me).wait_recv()
            to_pair(of_group, other).start()
            return carry

        lax.fori_loop(1, members // 2, step, 0)

    up = lax.rem(me + members, groups * members)
    down = lax.rem(me + (groups - 1) * members, groups * members)

    def when_low(s, run):
        pl.when(g - s >= 0)(lambda: run(jnp.maximum(g - s, 0)))

    def when_high(s, run):
        pl.when(g + s < groups)(lambda: run(jnp.minimum(g + s, groups - 1)))

    def relay_up(s):
        @pl.when((g - s >= 0) & (g + 1 < groups))
        def _():
            c = jnp.maximum(g - s, 0)
            gathered(c, m, ag_u.at[c], up).start()

    def relay_down(s):
        @pl.when((g + s < groups) & (g > 0))
        def _():
            c = jnp.minimum(g + s, groups - 1)
            gathered(c, m, ag_d.at[c], down).start()

    def arrive(c):
        gathered(c, m, ag_u.at[c], me).wait_recv()

    relay_up(0)
    relay_down(0)
    have(g)
    for s in range(1, groups):
        when_low(s, arrive)
        relay_up(s)
        when_low(s, have)
        when_high(s, arrive)
        relay_down(s)
        when_high(s, have)
        if s == 1:
            forward(g)
        else:
            when_low(s - 1, forward)
            when_high(s - 1, forward)
    if groups == 1:
        forward(g)
    else:
        when_low(groups - 1, forward)
        when_high(groups - 1, forward)

    def from_pair(i, carry):
        for c in range(groups):
            gathered(c, lax.rem(pair + 2 * i, members), ag_u.at[c], me).wait_recv()
        return carry

    lax.fori_loop(0, members // 2, from_pair, 0)

    out_rows = query_len // tps

    def project(of_tp):
        rows = pl.ds(pl.multiple_of(of_tp * out_rows, out_rows), out_rows)
        return jnp.dot(att[rows, :], w[...], preferred_element_type=F32)

    def sum_copy(of_tp, slot):
        return remote(ysend.at[of_tp], yrecv.at[slot], y_s.at[of_tp], y_r.at[slot], of_tp, "tp")

    for d in range(1, tps):
        to = lax.rem(my_tp + d, tps)
        ysend[to] = project(to).astype(BF16)
        sum_copy(to, my_tp).start()
    result = project(my_tp)
    for d in range(1, tps):
        source = lax.rem(my_tp + d, tps)
        sum_copy(source, source).wait_recv()
        result = result + yrecv[source].astype(F32)
    qo[...] = result.astype(BF16)
    store_query = local(qo, qo_h, 12)
    store_query.start()

    @pl.when(me == 0)
    def _():
        for p in range(1, pieces):
            for k, buf in enumerate((ak, av)):
                remote(buf.at[piece_rows(p)], buf.at[piece_rows(p)], an_s.at[p, k], an_r.at[k], p).wait_send()

    @pl.when(has_piece)
    def _():
        mine = piece_rows(m)

        @pl.when(g + 1 < groups)
        def _():
            for k, buf in enumerate((ak, av)):
                remote(buf.at[mine], buf.at[mine], an_u.at[k], an_r.at[k], me).wait_send()

        def spread_done(i, carry):
            other = lax.rem(m + i, members)

            @pl.when((g > 0) | (other > 0))
            def _():
                for k, buf in enumerate((ak, av)):
                    remote(buf.at[mine], buf.at[mine], an_rs.at[other, k], an_rr.at[m, k], me).wait_send()
            return carry

        lax.fori_loop(1, members, spread_done, 0)

    for d in range(1, groups):
        for copy in kv_copies(lax.rem(g + d, groups), g):
            copy.wait_send()

    def part_done(i, carry):
        for copy in part_copies(lax.rem(m + i, members), m):
            copy.wait_send()
        return carry

    lax.fori_loop(1, members, part_done, 0)
    for s in range(groups):
        @pl.when((g - s >= 0) & (g + 1 < groups))
        def _():
            c = jnp.maximum(g - s, 0)
            gathered(c, m, ag_u.at[c], up).wait_send()

        @pl.when((g + s < groups) & (g > 0))
        def _():
            c = jnp.minimum(g + s, groups - 1)
            gathered(c, m, ag_d.at[c], down).wait_send()

    def pair_done(i, carry):
        other = lax.rem(m + 2 * i, members)
        for c in range(groups):
            to_pair(c, other).wait_send()
        return carry

    lax.fori_loop(0, members // 2, pair_done, 0)

    def across_done(i, carry):
        other = lax.rem(m + 2 * i, members)
        for c in range(groups):
            gathered(c, m, ag_rs.at[c, other], me).wait_send()
        return carry

    lax.fori_loop(1, members // 2, across_done, 0)
    for d in range(1, tps):
        sum_copy(lax.rem(my_tp + d, tps), my_tp).wait_send()
    store_ctx.wait()
    store_query.wait()


def body(n_ctx, tps, ctx_queries, ctx_keys, ctx_values, query_queries, query_keys, query_values, out_weight):
    block, heads_wide = ctx_queries.shape
    kv_wide = ctx_keys.shape[1]
    kv_local = kv_wide // HD
    group = heads_wide // kv_wide
    share = query_keys.shape[0]
    query_len = query_queries.shape[0]
    groups = kv_local
    members = n_ctx // groups
    flat = group * query_len
    chunk = flat // members
    pieces = math.gcd(members, block // 16)
    query_rows = -(-groups * share // 128) * 128
    out_cols = out_weight.shape[1]
    out_rows = query_len // tps
    dims = (groups, members, tps, kv_local, group, block, share, query_len)
    any_spec = pl.BlockSpec(memory_space=pl.ANY)
    dma = pltpu.SemaphoreType.DMA
    vmem = pltpu.VMEM
    return pl.pallas_call(
        functools.partial(kernel, dims),
        out_shape=(
            jax.ShapeDtypeStruct((block, heads_wide), BF16),
            jax.ShapeDtypeStruct((out_rows, out_cols), BF16),
        ),
        in_specs=[any_spec] * 7,
        out_specs=(any_spec, any_spec),
        scratch_shapes=[
            vmem((block, heads_wide), BF16),
            vmem((block, kv_wide), BF16),
            vmem((block, kv_wide), BF16),
            vmem((block, kv_wide), BF16),
            vmem((block, kv_wide), BF16),
            vmem((query_len, group * HD), BF16),
            vmem(out_weight.shape, BF16),
            vmem((groups, block, HD), BF16),
            vmem((groups, block, HD), BF16),
            vmem((query_rows, HD), BF16),
            vmem((query_rows, HD), BF16),
            vmem((flat, 2 * HD), F32),
            vmem((flat, HD), F32),
            vmem((members, chunk, HD), BF16),
            vmem((members, 8, chunk), F32),
            vmem((members, chunk, HD), BF16),
            vmem((members, 8, chunk), F32),
            vmem((query_len, heads_wide), BF16),
            vmem((tps, out_rows, out_cols), BF16),
            vmem((tps, out_rows, out_cols), BF16),
            vmem((block, heads_wide), BF16),
            vmem((out_rows, out_cols), BF16),
            dma((13,)),
            dma((groups, 4)),
            dma((groups, 4)),
            dma((pieces, 2)),
            dma((2,)),
            dma((2,)),
            dma((members, 2)),
            dma((pieces, 2)),
            dma((members, 2)),
            dma((members, 2)),
            dma((groups, members)),
            dma((groups,)),
            dma((groups,)),
            dma((groups, members)),
            dma((groups, members)),
            dma((tps,)),
            dma((tps,)),
        ],
        compiler_params=pltpu.CompilerParams(
            collective_id=0, has_side_effects=True, vmem_limit_bytes=48 * 1024 * 1024
        ),
        cost_estimate=pl.CostEstimate(flops=3_000_000_000, bytes_accessed=8_000_000, transcendentals=4_000_000),
        name="star_attention",
    )(ctx_queries, ctx_keys, ctx_values, query_queries, query_keys, query_values, out_weight)


def solution(mesh):
    return jax.shard_map(
        functools.partial(body, mesh.shape["ctx"], mesh.shape["tp"]),
        mesh=mesh,
        in_specs=(
            P("ctx", "tp"),
            P("ctx", "tp"),
            P("ctx", "tp"),
            P(None, "tp"),
            P("ctx", "tp"),
            P("ctx", "tp"),
            P("tp", "ctx"),
        ),
        out_specs=(P("ctx", "tp"), P("tp", "ctx")),
        check_vma=False,
    )
```

```python
import functools
import math

import jax
import jax.numpy as jnp
from jax import lax
from jax.experimental import pallas as pl
from jax.experimental.pallas import tpu as pltpu
from jax.sharding import PartitionSpec as P

HD = 128
MESH = pl.DeviceIdType.MESH
COEF = HD ** (-0.5) * math.log2(math.e)
F32 = jnp.float32
BF16 = jnp.bfloat16
NEG = float("-inf")


def kernel(dims, cq_h, ck_h, cv_h, qq_h, qk_h, qv_h, w_h, co_h, qo_h, cq, ck, cv, ak, av, qq, w, kb, vb, kqb, vqb,
           acc, top, osend, lsend, orecv, lrecv, att, ysend, yrecv, co, qo, own_bias, query_bias, loc_sem, kv_s, kv_r, an_s, an_r, an_u,
           an_rs, an_rr, rs_s, rs_r, ag_r, ag_u, ag_d, ag_rs, ag_cs, y_s, y_r):
    groups, members, tps, kv_local, group, block, share, query_len = dims
    flat = group * query_len
    chunk = flat // members
    tile = min(256, chunk)
    pieces = math.gcd(members, block // 16)
    piece = block // pieces
    me = lax.axis_index("ctx")
    my_tp = lax.axis_index("tp")
    g = lax.div(me, members)
    m = lax.rem(me, members)
    pair = m + 1 - 2 * lax.rem(m, 2)

    def lanes(index):
        return pl.ds(pl.multiple_of(index * HD, HD), HD)

    def local(src, dst, i):
        return pltpu.make_async_copy(src, dst, loc_sem.at[i])

    def remote(src, dst, send, recv, to, axis="ctx"):
        return pltpu.make_async_remote_copy(src_ref=src, dst_ref=dst, send_sem=send, recv_sem=recv,
                                            device_id={axis: to}, device_id_type=MESH)

    wide = pl.ds(pl.multiple_of(g * (group * HD), HD), group * HD)
    own_rows = pl.ds(pl.multiple_of(g * share, share), share)
    loads = [
        local(qq_h.at[:, wide], qq, 0),
        local(ck_h.at[:, lanes(g)], kb.at[g], 1),
        local(cv_h.at[:, lanes(g)], vb.at[g], 2),
        local(ck_h, ck, 3),
        local(cv_h, cv, 4),
        local(cq_h, cq, 5),
        local(w_h, w, 6),
        local(qk_h.at[:, lanes(g)], kqb.at[own_rows], 7),
        local(qv_h.at[:, lanes(g)], vqb.at[own_rows], 8),
    ]
    if kqb.shape[0] > groups * share:
        kqb[...] = jnp.zeros_like(kqb)
        vqb[...] = jnp.zeros_like(vqb)
    for load in loads:
        load.start()

    @pl.when(me == 0)
    def _():
        local(ck_h, ak, 9).start()
        local(cv_h, av, 10).start()

    barrier = pltpu.get_barrier_semaphore()

    def greet_group(i, carry):
        to = g * members + lax.rem(m + i, members)
        pl.semaphore_signal(barrier, inc=1, device_id={"ctx": to}, device_id_type=MESH)
        return carry

    lax.fori_loop(1, members, greet_group, 0)
    for d in range(1, groups):
        to = lax.rem(g + d, groups) * members + m
        pl.semaphore_signal(barrier, inc=1, device_id={"ctx": to}, device_id_type=MESH)
    for d in range(1, tps):
        pl.semaphore_signal(barrier, inc=1, device_id={"tp": lax.rem(my_tp + d, tps)}, device_id_type=MESH)
    pl.semaphore_wait(barrier, members - 1 + groups - 1 + tps - 1)

    def piece_rows(p):
        return pl.ds(pl.multiple_of(p * piece, piece), piece)

    @pl.when(me == 0)
    def _():
        local(ck_h, ak, 9).wait()
        local(cv_h, av, 10).wait()
        for p in range(1, pieces):
            for k, buf in enumerate((ak, av)):
                remote(buf.at[piece_rows(p)], buf.at[piece_rows(p)], an_s.at[p, k], an_r.at[k], p).start()

    def kv_copies(to_group, slot):
        to = to_group * members + m
        rows = pl.ds(pl.multiple_of(slot * share, share), share)
        return [
            remote(ck_h.at[:, lanes(to_group)], kb.at[slot], kv_s.at[to_group, 0], kv_r.at[slot, 0], to),
            remote(cv_h.at[:, lanes(to_group)], vb.at[slot], kv_s.at[to_group, 1], kv_r.at[slot, 1], to),
            remote(qk_h.at[:, lanes(to_group)], kqb.at[rows], kv_s.at[to_group, 2], kv_r.at[slot, 2], to),
            remote(qv_h.at[:, lanes(to_group)], vqb.at[rows], kv_s.at[to_group, 3], kv_r.at[slot, 3], to),
        ]

    for d in range(1, groups):
        for copy in kv_copies(lax.rem(g + d, groups), g):
            copy.start()

    at = lax.broadcasted_iota(jnp.int32, own_bias.shape, 0)
    own_bias[...] = jnp.where(lax.broadcasted_iota(jnp.int32, own_bias.shape, 1) <= at, 0.0, NEG)
    col = lax.broadcasted_iota(jnp.int32, (1, query_bias.shape[1]), 1)
    position = (lax.div(col, share) * members + m) * share + lax.rem(col, share)
    position = jnp.where(col < groups * share, position, query_len)
    at = lax.broadcasted_iota(jnp.int32, query_bias.shape, 0)
    query_bias[...] = jnp.where(at >= position, 0.0, NEG)

    def attend(first_row, first, slot, with_query):
        head = lax.div(first_row, query_len)
        row = lax.rem(first_row, query_len)
        q = qq[pl.ds(pl.multiple_of(row, tile), tile), lanes(head)]
        keys, values = kb[slot], vb[slot]
        if with_query:
            keys = jnp.concatenate([keys, kqb[...]], 0)
            values = jnp.concatenate([values, vqb[...]], 0)
        values = jnp.concatenate([values, jnp.ones_like(values)], 1)
        s = lax.dot_general(q, keys, (((1,), (1,)), ((), ())), preferred_element_type=F32) * COEF
        if with_query:
            bias = query_bias[pl.ds(pl.multiple_of(row, tile), tile), :]
            s = jnp.concatenate([s[:, :block], s[:, block:] + bias], 1)
        rows = pl.ds(pl.multiple_of(first_row, tile), tile)
        high = jnp.max(s, axis=1, keepdims=True)
        if not first:
            before = top[rows, :]
            high = jnp.maximum(high, before[:, :1])
        p = jnp.exp2(s - high).astype(BF16)
        o = jnp.dot(p, values, preferred_element_type=F32)
        if not first:
            o = o + acc[rows, :] * jnp.exp2(before[:, :1] - high)
        acc[rows, :] = o
        top[rows, :] = jnp.broadcast_to(high, (tile, HD))

    def sweep(slot, first):
        def step(t, carry):
            attend(t * tile, first, slot, False)
            return carry

        lax.fori_loop(0, flat // tile, step, 0, unroll=2)

    for i in (0, 1, 2):
        loads[i].wait()
    if groups > 1:
        sweep(g, True)

    for i in (3, 4, 5, 6, 7, 8):
        loads[i].wait()
    not_root = me > 0
    has_piece = m < pieces

    @pl.when(has_piece)
    def _():
        mine = piece_rows(m)
        for k, buf in enumerate((ak, av)):
            @pl.when(not_root)
            def _():
                remote(buf.at[mine], buf.at[mine], an_u.at[k], an_r.at[k], me).wait_recv()

            @pl.when(g + 1 < groups)
            def _():
                remote(buf.at[mine], buf.at[mine], an_u.at[k], an_r.at[k], lax.rem(me + members, groups * members)).start()

        def spread(i, carry):
            other = lax.rem(m + i, members)

            @pl.when((g > 0) | (other > 0))
            def _():
                for k, buf in enumerate((ak, av)):
                    remote(buf.at[mine], buf.at[mine], an_rs.at[other, k], an_rr.at[m, k], g * members + other).start()
            return carry

        lax.fori_loop(1, members, spread, 0)

    anchor_bias = jnp.where(not_root, 0.0, NEG)

    def context_head(h):
        kv = lanes(lax.div(h, group))
        q = cq[:, lanes(h)]
        keys = jnp.concatenate([ak[:, kv], ck[:, kv]], 0)
        values = jnp.concatenate([av[:, kv], cv[:, kv]], 0)
        values = jnp.concatenate([values, jnp.ones_like(values)], 1)
        s = lax.dot_general(q, keys, (((1,), (1,)), ((), ())), preferred_element_type=F32) * COEF
        s = jnp.concatenate([s[:, :block] + anchor_bias, s[:, block:] + own_bias[...]], 1)
        p = jnp.exp2(s - jnp.max(s, axis=1, keepdims=True)).astype(BF16)
        o = jnp.dot(p, values, preferred_element_type=F32)
        co[:, lanes(h)] = (o[:, :HD] / o[:, HD:]).astype(BF16)

    heads = kv_local * group

    def context_heads(stage):
        first, end = stage * heads // groups, (stage + 1) * heads // groups

        def step(h, carry):
            context_head(h)
            return carry

        lax.fori_loop(first, end, step, 0, unroll=2)

    for d in range(1, groups):
        slot = lax.rem(g + d, groups)
        for copy in kv_copies(slot, slot):
            copy.wait_recv()
        if d < groups - 1:
            sweep(slot, False)
    last = lax.rem(g + groups - 1, groups)

    def part(to):
        rows = pl.ds(pl.multiple_of(to * chunk, chunk), chunk)
        total = acc[rows, HD:]
        return acc[rows, :HD] / total, top[rows, :] + jnp.log2(total)

    def attend_chunk(to):
        for t in range(chunk // tile):
            attend(to * chunk + t * tile, groups == 1, last, True)

    def part_copies(to, slot):
        target = g * members + to
        return [
            remote(osend.at[to], orecv.at[slot], rs_s.at[to, 0], rs_r.at[slot, 0], target),
            remote(lsend.at[to], lrecv.at[slot], rs_s.at[to, 1], rs_r.at[slot, 1], target),
        ]

    def send_part(i, carry):
        to = lax.rem(m + i, members)
        attend_chunk(to)
        out, lse = part(to)
        osend[to] = out.astype(BF16)
        lsend[to] = jnp.transpose(lse)[:8, :]
        for copy in part_copies(to, m):
            copy.start()
        return carry

    lax.fori_loop(1, members, send_part, 0)
    attend_chunk(m)

    @pl.when(not_root)
    def _():
        def gather(p, carry):
            @pl.when(p != m)
            def _():
                for k, buf in enumerate((ak, av)):
                    remote(buf.at[piece_rows(p)], buf.at[piece_rows(p)], an_u.at[k], an_rr.at[p, k], me).wait_recv()
            return carry

        lax.fori_loop(0, pieces, gather, 0)

    context_heads(0)

    def wait_part(i, carry):
        for copy in part_copies(lax.rem(m + i, members), lax.rem(m + i, members)):
            copy.wait_recv()
        return carry

    lax.fori_loop(1, members, wait_part, 0)

    def lse_of(i):
        row = lrecv[lax.rem(m + i, members)][:1, :]
        return jnp.transpose(jnp.broadcast_to(row, (HD, chunk)))

    own, own_lse = part(m)
    highest = lax.fori_loop(1, members, lambda i, high: jnp.maximum(high, lse_of(i)), own_lse)
    own_weight = jnp.exp2(own_lse - highest)

    def combine(i, carry):
        total, summed = carry
        weight = jnp.exp2(lse_of(i) - highest)
        return total + weight, summed + weight * orecv[lax.rem(m + i, members)].astype(F32)

    total, summed = lax.fori_loop(1, members, combine, (own_weight, own_weight * own))

    def place(of_group, of_member):
        start = of_member * chunk
        row = pl.multiple_of(lax.rem(start, query_len), chunk)
        return att.at[pl.ds(row, chunk), lanes(of_group * group + lax.div(start, query_len))]

    place(g, m)[...] = (summed / total).astype(BF16)

    def gathered(of_group, of_member, send, to):
        where = place(of_group, of_member)
        return remote(where, where, send, ag_r.at[of_group, of_member], to)

    def to_pair(of_group, of_member):
        return gathered(of_group, of_member, ag_cs.at[of_group, of_member], g * members + pair)

    def have(of_group):
        def across(i, carry):
            other = lax.rem(m + 2 * i, members)
            gathered(of_group, m, ag_rs.at[of_group, other], g * members + other).start()
            return carry

        lax.fori_loop(1, members // 2, across, 0)
        to_pair(of_group, m).start()

    def forward(of_group):
        def step(i, carry):
            other = lax.rem(m + 2 * i, members)
            gathered(of_group, other, ag_cs.at[of_group, other], me).wait_recv()
            to_pair(of_group, other).start()
            return carry

        lax.fori_loop(1, members // 2, step, 0)

    up = lax.rem(me + members, groups * members)
    down = lax.rem(me + (groups - 1) * members, groups * members)

    def when_low(s, run):
        pl.when(g - s >= 0)(lambda: run(jnp.maximum(g - s, 0)))

    def when_high(s, run):
        pl.when(g + s < groups)(lambda: run(jnp.minimum(g + s, groups - 1)))

    def relay_up(s):
        @pl.when((g - s >= 0) & (g + 1 < groups))
        def _():
            c = jnp.maximum(g - s, 0)
            gathered(c, m, ag_u.at[c], up).start()

    def relay_down(s):
        @pl.when((g + s < groups) & (g > 0))
        def _():
            c = jnp.minimum(g + s, groups - 1)
            gathered(c, m, ag_d.at[c], down).start()

    def arrive(c):
        gathered(c, m, ag_u.at[c], me).wait_recv()

    relay_up(0)
    relay_down(0)
    have(g)
    for s in range(1, groups):
        context_heads(s)
        when_low(s, arrive)
        relay_up(s)
        when_low(s, have)
        when_high(s, arrive)
        relay_down(s)
        when_high(s, have)
        if s == 1:
            forward(g)
        else:
            when_low(s - 1, forward)
            when_high(s - 1, forward)
    if groups == 1:
        forward(g)
    else:
        when_low(groups - 1, forward)
        when_high(groups - 1, forward)

    store_ctx = local(co, co_h, 11)
    store_ctx.start()

    def from_pair(i, carry):
        for c in range(groups):
            gathered(c, lax.rem(pair + 2 * i, members), ag_u.at[c], me).wait_recv()
        return carry

    lax.fori_loop(0, members // 2, from_pair, 0)

    out_rows = query_len // tps

    def project(of_tp):
        rows = pl.ds(pl.multiple_of(of_tp * out_rows, out_rows), out_rows)
        return jnp.dot(att[rows, :], w[...], preferred_element_type=F32)

    def sum_copy(of_tp, slot):
        return remote(ysend.at[of_tp], yrecv.at[slot], y_s.at[of_tp], y_r.at[slot], of_tp, "tp")

    for d in range(1, tps):
        to = lax.rem(my_tp + d, tps)
        ysend[to] = project(to).astype(BF16)
        sum_copy(to, my_tp).start()
    result = project(my_tp)
    for d in range(1, tps):
        source = lax.rem(my_tp + d, tps)
        sum_copy(source, source).wait_recv()
        result = result + yrecv[source].astype(F32)
    qo[...] = result.astype(BF16)
    store_query = local(qo, qo_h, 12)
    store_query.start()

    @pl.when(me == 0)
    def _():
        for p in range(1, pieces):
            for k, buf in enumerate((ak, av)):
                remote(buf.at[piece_rows(p)], buf.at[piece_rows(p)], an_s.at[p, k], an_r.at[k], p).wait_send()

    @pl.when(has_piece)
    def _():
        mine = piece_rows(m)

        @pl.when(g + 1 < groups)
        def _():
            for k, buf in enumerate((ak, av)):
                remote(buf.at[mine], buf.at[mine], an_u.at[k], an_r.at[k], me).wait_send()

        def spread_done(i, carry):
            other = lax.rem(m + i, members)

            @pl.when((g > 0) | (other > 0))
            def _():
                for k, buf in enumerate((ak, av)):
                    remote(buf.at[mine], buf.at[mine], an_rs.at[other, k], an_rr.at[m, k], me).wait_send()
            return carry

        lax.fori_loop(1, members, spread_done, 0)

    for d in range(1, groups):
        for copy in kv_copies(lax.rem(g + d, groups), g):
            copy.wait_send()

    def part_done(i, carry):
        for copy in part_copies(lax.rem(m + i, members), m):
            copy.wait_send()
        return carry

    lax.fori_loop(1, members, part_done, 0)
    for s in range(groups):
        @pl.when((g - s >= 0) & (g + 1 < groups))
        def _():
            c = jnp.maximum(g - s, 0)
            gathered(c, m, ag_u.at[c], up).wait_send()

        @pl.when((g + s < groups) & (g > 0))
        def _():
            c = jnp.minimum(g + s, groups - 1)
            gathered(c, m, ag_d.at[c], down).wait_send()

    def pair_done(i, carry):
        other = lax.rem(m + 2 * i, members)
        for c in range(groups):
            to_pair(c, other).wait_send()
        return carry

    lax.fori_loop(0, members // 2, pair_done, 0)

    def across_done(i, carry):
        other = lax.rem(m + 2 * i, members)
        for c in range(groups):
            gathered(c, m, ag_rs.at[c, other], me).wait_send()
        return carry

    lax.fori_loop(1, members // 2, across_done, 0)
    for d in range(1, tps):
        sum_copy(lax.rem(my_tp + d, tps), my_tp).wait_send()
    store_ctx.wait()
    store_query.wait()


def body(n_ctx, tps, ctx_queries, ctx_keys, ctx_values, query_queries, query_keys, query_values, out_weight):
    block, heads_wide = ctx_queries.shape
    kv_wide = ctx_keys.shape[1]
    kv_local = kv_wide // HD
    group = heads_wide // kv_wide
    share = query_keys.shape[0]
    query_len = query_queries.shape[0]
    groups = kv_local
    members = n_ctx // groups
    flat = group * query_len
    chunk = flat // members
    pieces = math.gcd(members, block // 16)
    query_rows = -(-groups * share // 128) * 128
    out_cols = out_weight.shape[1]
    out_rows = query_len // tps
    dims = (groups, members, tps, kv_local, group, block, share, query_len)
    any_spec = pl.BlockSpec(memory_space=pltpu.HBM)
    dma = pltpu.SemaphoreType.DMA
    vmem = pltpu.VMEM
    return pl.pallas_call(
        functools.partial(kernel, dims),
        out_shape=(
            jax.ShapeDtypeStruct((block, heads_wide), BF16),
            jax.ShapeDtypeStruct((out_rows, out_cols), BF16),
        ),
        in_specs=[any_spec] * 7,
        out_specs=(any_spec, any_spec),
        scratch_shapes=[
            vmem((block, heads_wide), BF16),
            vmem((block, kv_wide), BF16),
            vmem((block, kv_wide), BF16),
            vmem((block, kv_wide), BF16),
            vmem((block, kv_wide), BF16),
            vmem((query_len, group * HD), BF16),
            vmem(out_weight.shape, BF16),
            vmem((groups, block, HD), BF16),
            vmem((groups, block, HD), BF16),
            vmem((query_rows, HD), BF16),
            vmem((query_rows, HD), BF16),
            vmem((flat, 2 * HD), F32),
            vmem((flat, HD), F32),
            vmem((members, chunk, HD), BF16),
            vmem((members, 8, chunk), F32),
            vmem((members, chunk, HD), BF16),
            vmem((members, 8, chunk), F32),
            vmem((query_len, heads_wide), BF16),
            vmem((tps, out_rows, out_cols), BF16),
            vmem((tps, out_rows, out_cols), BF16),
            vmem((block, heads_wide), BF16),
            vmem((out_rows, out_cols), BF16),
            vmem((block, block), F32),
            vmem((query_len, query_rows), F32),
            dma((13,)),
            dma((groups, 4)),
            dma((groups, 4)),
            dma((pieces, 2)),
            dma((2,)),
            dma((2,)),
            dma((members, 2)),
            dma((pieces, 2)),
            dma((members, 2)),
            dma((members, 2)),
            dma((groups, members)),
            dma((groups,)),
            dma((groups,)),
            dma((groups, members)),
            dma((groups, members)),
            dma((tps,)),
            dma((tps,)),
        ],
        compiler_params=pltpu.CompilerParams(
            collective_id=0, has_side_effects=True, vmem_limit_bytes=64 * 1024 * 1024
        ),
        cost_estimate=pl.CostEstimate(flops=3_000_000_000, bytes_accessed=8_000_000, transcendentals=4_000_000),
        name="star_attention",
    )(ctx_queries, ctx_keys, ctx_values, query_queries, query_keys, query_values, out_weight)


def solution(mesh):
    return jax.shard_map(
        functools.partial(body, mesh.shape["ctx"], mesh.shape["tp"]),
        mesh=mesh,
        in_specs=(
            P("ctx", "tp"),
            P("ctx", "tp"),
            P("ctx", "tp"),
            P(None, "tp"),
            P("ctx", "tp"),
            P("ctx", "tp"),
            P("tp", "ctx"),
        ),
        out_specs=(P("ctx", "tp"), P("tp", "ctx")),
        check_vma=False,
    )
```

```python
import functools
import math

import jax
import jax.numpy as jnp
from jax import lax
from jax.experimental import pallas as pl
from jax.experimental.pallas import tpu as pltpu
from jax.sharding import PartitionSpec as P

HD = 128
MESH = pl.DeviceIdType.MESH
COEF = HD ** (-0.5) * math.log2(math.e)
F32 = jnp.float32
BF16 = jnp.bfloat16
NEG = float("-inf")


def kernel(dims, cq_h, ck_h, cv_h, qq_h, qk_h, qv_h, w_h, co_h, qo_h, cq, ck, cv, ak, av, qq, w, kb, vb, kqb, vqb,
           acc, top, osend, lsend, orecv, lrecv, att, ysend, yrecv, co, qo, own_bias, query_bias, loc_sem, kv_s, kv_r, an_s, an_r, an_u,
           an_rs, an_rr, rs_s, rs_r, ag_r, ag_u, ag_d, ag_rs, ag_cs, y_s, y_r):
    groups, members, tps, kv_local, group, block, share, query_len = dims
    flat = group * query_len
    chunk = flat // members
    tile = min(256, chunk)
    pieces = math.gcd(members, block // 16)
    piece = block // pieces
    me = lax.axis_index("ctx")
    my_tp = lax.axis_index("tp")
    g = lax.div(me, members)
    m = lax.rem(me, members)
    pair = m + 1 - 2 * lax.rem(m, 2)

    def lanes(index):
        return pl.ds(pl.multiple_of(index * HD, HD), HD)

    def local(src, dst, i):
        return pltpu.make_async_copy(src, dst, loc_sem.at[i])

    def remote(src, dst, send, recv, to, axis="ctx"):
        return pltpu.make_async_remote_copy(src_ref=src, dst_ref=dst, send_sem=send, recv_sem=recv,
                                            device_id={axis: to}, device_id_type=MESH)

    wide = pl.ds(pl.multiple_of(g * (group * HD), HD), group * HD)
    own_rows = pl.ds(pl.multiple_of(g * share, share), share)
    loads = [
        local(qq_h.at[:, wide], qq, 0),
        local(ck_h.at[:, lanes(g)], kb.at[g], 1),
        local(cv_h.at[:, lanes(g)], vb.at[g], 2),
        local(ck_h, ck, 3),
        local(cv_h, cv, 4),
        local(cq_h, cq, 5),
        local(w_h, w, 6),
        local(qk_h.at[:, lanes(g)], kqb.at[own_rows], 7),
        local(qv_h.at[:, lanes(g)], vqb.at[own_rows], 8),
    ]
    if kqb.shape[0] > groups * share:
        kqb[...] = jnp.zeros_like(kqb)
        vqb[...] = jnp.zeros_like(vqb)
    for load in loads:
        load.start()

    @pl.when(me == 0)
    def _():
        local(ck_h, ak, 9).start()
        local(cv_h, av, 10).start()

    barrier = pltpu.get_barrier_semaphore()

    def greet_group(i, carry):
        to = g * members + lax.rem(m + i, members)
        pl.semaphore_signal(barrier, inc=1, device_id={"ctx": to}, device_id_type=MESH)
        return carry

    lax.fori_loop(1, members, greet_group, 0)
    for d in range(1, groups):
        to = lax.rem(g + d, groups) * members + m
        pl.semaphore_signal(barrier, inc=1, device_id={"ctx": to}, device_id_type=MESH)
    for d in range(1, tps):
        pl.semaphore_signal(barrier, inc=1, device_id={"tp": lax.rem(my_tp + d, tps)}, device_id_type=MESH)
    pl.semaphore_wait(barrier, members - 1 + groups - 1 + tps - 1)

    def piece_rows(p):
        return pl.ds(pl.multiple_of(p * piece, piece), piece)

    @pl.when(me == 0)
    def _():
        local(ck_h, ak, 9).wait()
        local(cv_h, av, 10).wait()
        for p in range(1, pieces):
            for k, buf in enumerate((ak, av)):
                remote(buf.at[piece_rows(p)], buf.at[piece_rows(p)], an_s.at[p, k], an_r.at[k], p).start()

    def kv_copies(to_group, slot):
        to = to_group * members + m
        rows = pl.ds(pl.multiple_of(slot * share, share), share)
        return [
            remote(ck_h.at[:, lanes(to_group)], kb.at[slot], kv_s.at[to_group, 0], kv_r.at[slot, 0], to),
            remote(cv_h.at[:, lanes(to_group)], vb.at[slot], kv_s.at[to_group, 1], kv_r.at[slot, 1], to),
            remote(qk_h.at[:, lanes(to_group)], kqb.at[rows], kv_s.at[to_group, 2], kv_r.at[slot, 2], to),
            remote(qv_h.at[:, lanes(to_group)], vqb.at[rows], kv_s.at[to_group, 3], kv_r.at[slot, 3], to),
        ]

    for d in range(1, groups):
        for copy in kv_copies(lax.rem(g + d, groups), g):
            copy.start()

    at = lax.broadcasted_iota(jnp.int32, own_bias.shape, 0)
    own_bias[...] = jnp.where(lax.broadcasted_iota(jnp.int32, own_bias.shape, 1) <= at, 0.0, NEG)
    col = lax.broadcasted_iota(jnp.int32, (1, query_bias.shape[1]), 1)
    position = (lax.div(col, share) * members + m) * share + lax.rem(col, share)
    position = jnp.where(col < groups * share, position, query_len)
    at = lax.broadcasted_iota(jnp.int32, query_bias.shape, 0)
    query_bias[...] = jnp.where(at >= position, 0.0, NEG)

    def attend(first_row, first, slot, with_query):
        head = lax.div(first_row, query_len)
        row = lax.rem(first_row, query_len)
        q = qq[pl.ds(pl.multiple_of(row, tile), tile), lanes(head)]
        keys, values = kb[slot], vb[slot]
        if with_query:
            keys = jnp.concatenate([keys, kqb[...]], 0)
            values = jnp.concatenate([values, vqb[...]], 0)
        values = jnp.concatenate([values, jnp.ones_like(values)], 1)
        s = lax.dot_general(q, keys, (((1,), (1,)), ((), ())), preferred_element_type=F32) * COEF
        if with_query:
            bias = query_bias[pl.ds(pl.multiple_of(row, tile), tile), :]
            s = jnp.concatenate([s[:, :block], s[:, block:] + bias], 1)
        rows = pl.ds(pl.multiple_of(first_row, tile), tile)
        high = jnp.max(s, axis=1, keepdims=True)
        if not first:
            before = top[rows, :]
            high = jnp.maximum(high, before[:, :1])
        p = jnp.exp2(s - high).astype(BF16)
        o = jnp.dot(p, values, preferred_element_type=F32)
        if not first:
            o = o + acc[rows, :] * jnp.exp2(before[:, :1] - high)
        acc[rows, :] = o
        top[rows, :] = jnp.broadcast_to(high, (tile, HD))

    def sweep(slot, first):
        def step(t, carry):
            attend(t * tile, first, slot, False)
            return carry

        lax.fori_loop(0, flat // tile, step, 0, unroll=2)

    for i in (0, 1, 2):
        loads[i].wait()
    if groups > 1:
        sweep(g, True)

    for i in (3, 4, 5, 6, 7, 8):
        loads[i].wait()
    not_root = me > 0
    has_piece = m < pieces

    @pl.when(has_piece)
    def _():
        mine = piece_rows(m)
        for k, buf in enumerate((ak, av)):
            @pl.when(not_root)
            def _():
                remote(buf.at[mine], buf.at[mine], an_u.at[k], an_r.at[k], me).wait_recv()

            @pl.when(g + 1 < groups)
            def _():
                remote(buf.at[mine], buf.at[mine], an_u.at[k], an_r.at[k], lax.rem(me + members, groups * members)).start()

        def spread(i, carry):
            other = lax.rem(m + i, members)

            @pl.when((g > 0) | (other > 0))
            def _():
                for k, buf in enumerate((ak, av)):
                    remote(buf.at[mine], buf.at[mine], an_rs.at[other, k], an_rr.at[m, k], g * members + other).start()
            return carry

        lax.fori_loop(1, members, spread, 0)

    anchor_bias = jnp.where(not_root, 0.0, NEG)

    def context_head(h):
        kv = lanes(lax.div(h, group))
        q = cq[:, lanes(h)]
        keys = jnp.concatenate([ak[:, kv], ck[:, kv]], 0)
        values = jnp.concatenate([av[:, kv], cv[:, kv]], 0)
        values = jnp.concatenate([values, jnp.ones_like(values)], 1)
        s = lax.dot_general(q, keys, (((1,), (1,)), ((), ())), preferred_element_type=F32) * COEF
        s = jnp.concatenate([s[:, :block] + anchor_bias, s[:, block:] + own_bias[...]], 1)
        p = jnp.exp2(s - jnp.max(s, axis=1, keepdims=True)).astype(BF16)
        o = jnp.dot(p, values, preferred_element_type=F32)
        co[:, lanes(h)] = (o[:, :HD] / o[:, HD:]).astype(BF16)

    heads = kv_local * group

    def context_heads(stage):
        first, end = stage * heads // groups, (stage + 1) * heads // groups

        def step(h, carry):
            context_head(h)
            return carry

        lax.fori_loop(first, end, step, 0, unroll=2)

    for d in range(1, groups):
        slot = lax.rem(g + d, groups)
        for copy in kv_copies(slot, slot):
            copy.wait_recv()
        if d < groups - 1:
            sweep(slot, False)
    last = lax.rem(g + groups - 1, groups)

    def part(to):
        rows = pl.ds(pl.multiple_of(to * chunk, chunk), chunk)
        total = acc[rows, HD:]
        return acc[rows, :HD] / total, top[rows, :] + jnp.log2(total)

    def attend_chunk(to):
        for t in range(chunk // tile):
            attend(to * chunk + t * tile, groups == 1, last, True)

    def part_copies(to, slot):
        target = g * members + to
        return [
            remote(osend.at[to], orecv.at[slot], rs_s.at[to, 0], rs_r.at[slot, 0], target),
            remote(lsend.at[to], lrecv.at[slot], rs_s.at[to, 1], rs_r.at[slot, 1], target),
        ]

    def send_part(i, carry):
        to = jnp.where(i < members - 1, lax.rem(m - lax.rem(m, 2) + 1 + i, members), pair)
        attend_chunk(to)
        out, lse = part(to)
        osend[to] = out.astype(BF16)
        lsend[to] = jnp.transpose(lse)[:8, :]
        for copy in part_copies(to, m):
            copy.start()
        return carry

    lax.fori_loop(1, members, send_part, 0)
    attend_chunk(m)

    @pl.when(not_root)
    def _():
        def gather(p, carry):
            @pl.when(p != m)
            def _():
                for k, buf in enumerate((ak, av)):
                    remote(buf.at[piece_rows(p)], buf.at[piece_rows(p)], an_u.at[k], an_rr.at[p, k], me).wait_recv()
            return carry

        lax.fori_loop(0, pieces, gather, 0)

    context_heads(0)

    def wait_part(i, carry):
        for copy in part_copies(lax.rem(m + i, members), lax.rem(m + i, members)):
            copy.wait_recv()
        return carry

    lax.fori_loop(1, members, wait_part, 0)

    def lse_of(i):
        row = lrecv[lax.rem(m + i, members)][:1, :]
        return jnp.transpose(jnp.broadcast_to(row, (HD, chunk)))

    own, own_lse = part(m)
    highest = lax.fori_loop(1, members, lambda i, high: jnp.maximum(high, lse_of(i)), own_lse)
    own_weight = jnp.exp2(own_lse - highest)

    def combine(i, carry):
        total, summed = carry
        weight = jnp.exp2(lse_of(i) - highest)
        return total + weight, summed + weight * orecv[lax.rem(m + i, members)].astype(F32)

    total, summed = lax.fori_loop(1, members, combine, (own_weight, own_weight * own))

    half = chunk // 2
    mates = members // 2

    def place(of_group, of_member, part_of):
        start = of_member * chunk
        row = pl.multiple_of(lax.rem(start, query_len) + part_of * half, half)
        return att.at[pl.ds(row, half), lanes(of_group * group + lax.div(start, query_len))]

    attended = (summed / total).astype(BF16)
    for h in range(2):
        place(g, m, h)[...] = attended[h * half:(h + 1) * half]

    def gathered(of_group, of_member, part_of, send, to):
        where = place(of_group, of_member, part_of)
        return remote(where, where, send, ag_r.at[of_group, of_member, part_of], to)

    def mate(i):
        return lax.rem(m + 2 * i, members)

    def over_mates(first, run):
        def step(i, carry):
            run(mate(i))
            return carry

        lax.fori_loop(first, mates, step, 0)

    up = lax.rem(me + members, groups * members)
    down = lax.rem(me + (groups - 1) * members, groups * members)

    def to_pair(c, i, h):
        return gathered(c, i, h, ag_cs.at[c, i, h], g * members + pair)

    def across(c, h, other):
        return gathered(c, m, h, ag_rs.at[c, other, h], g * members + other)

    def go_up(c, i, h):
        return gathered(c, i, h, ag_u.at[c, i, h], up)

    def go_down(c, i, h):
        return gathered(c, i, h, ag_d.at[c, i, h], down)

    def arrive(c, i, h):
        gathered(c, i, h, ag_cs.at[c, i, h], me).wait_recv()

    def relay_up(c, i, h):
        pl.when(g + 1 < groups)(lambda: go_up(c, i, h).start())

    def relay_down(c, i, h):
        pl.when(g > 0)(lambda: go_down(c, i, h).start())

    def when_low(s, run):
        pl.when(g - s >= 0)(lambda: run(jnp.maximum(g - s, 0)))

    def when_high(s, run):
        pl.when(g + s < groups)(lambda: run(jnp.minimum(g + s, groups - 1)))

    def from_column(relay):
        def run(c):
            arrive(c, m, 0)
            relay(c, m, 0)
            over_mates(1, lambda other: across(c, 0, other).start())
            to_pair(c, m, 0).start()

            def second(i):
                arrive(c, i, 1)
                relay(c, i, 1)
                to_pair(c, i, 1).start()

            over_mates(0, second)

        return run

    def from_row(c):
        def first_half(i):
            arrive(c, i, 0)
            to_pair(c, i, 0).start()

        over_mates(1, first_half)

    over_mates(1, lambda other: across(g, 1, other).start())
    for h in range(2):
        relay_up(g, m, h)
        relay_down(g, m, h)
    over_mates(1, lambda other: across(g, 0, other).start())
    for h in range(2):
        to_pair(g, m, h).start()

    def second_half(i):
        arrive(g, i, 1)
        relay_up(g, i, 1)
        relay_down(g, i, 1)
        to_pair(g, i, 1).start()

    over_mates(1, second_half)
    for s in range(1, groups):
        context_heads(s)
        when_low(s, from_column(relay_up))
        when_high(s, from_column(relay_down))
        if s == 1:
            from_row(g)
        else:
            when_low(s - 1, from_row)
            when_high(s - 1, from_row)
    if groups == 1:
        from_row(g)
    else:
        when_low(groups - 1, from_row)
        when_high(groups - 1, from_row)
    store_ctx = local(co, co_h, 11)
    store_ctx.start()

    def from_pair(i, carry):
        for c in range(groups):
            for h in range(2):
                arrive(c, lax.rem(pair + 2 * i, members), h)
        return carry

    lax.fori_loop(0, mates, from_pair, 0)

    out_rows = query_len // tps

    def project(of_tp):
        rows = pl.ds(pl.multiple_of(of_tp * out_rows, out_rows), out_rows)
        return jnp.dot(att[rows, :], w[...], preferred_element_type=F32)

    def sum_copy(of_tp, slot):
        return remote(ysend.at[of_tp], yrecv.at[slot], y_s.at[of_tp], y_r.at[slot], of_tp, "tp")

    for d in range(1, tps):
        to = lax.rem(my_tp + d, tps)
        ysend[to] = project(to).astype(BF16)
        sum_copy(to, my_tp).start()
    result = project(my_tp)
    for d in range(1, tps):
        source = lax.rem(my_tp + d, tps)
        sum_copy(source, source).wait_recv()
        result = result + yrecv[source].astype(F32)
    qo[...] = result.astype(BF16)
    store_query = local(qo, qo_h, 12)
    store_query.start()

    @pl.when(me == 0)
    def _():
        for p in range(1, pieces):
            for k, buf in enumerate((ak, av)):
                remote(buf.at[piece_rows(p)], buf.at[piece_rows(p)], an_s.at[p, k], an_r.at[k], p).wait_send()

    @pl.when(has_piece)
    def _():
        mine = piece_rows(m)

        @pl.when(g + 1 < groups)
        def _():
            for k, buf in enumerate((ak, av)):
                remote(buf.at[mine], buf.at[mine], an_u.at[k], an_r.at[k], me).wait_send()

        def spread_done(i, carry):
            other = lax.rem(m + i, members)

            @pl.when((g > 0) | (other > 0))
            def _():
                for k, buf in enumerate((ak, av)):
                    remote(buf.at[mine], buf.at[mine], an_rs.at[other, k], an_rr.at[m, k], me).wait_send()
            return carry

        lax.fori_loop(1, members, spread_done, 0)

    for d in range(1, groups):
        for copy in kv_copies(lax.rem(g + d, groups), g):
            copy.wait_send()

    def part_done(i, carry):
        for copy in part_copies(lax.rem(m + i, members), m):
            copy.wait_send()
        return carry

    lax.fori_loop(1, members, part_done, 0)

    def column_done(c, towards, can):
        @pl.when(can)
        def _():
            towards(c, m, 0).wait_send()
            over_mates(0, lambda i: towards(c, i, 1).wait_send())

    for c in range(groups):
        column_done(c, go_up, (c <= g) & (g + 1 < groups))
        column_done(c, go_down, (c >= g) & (g > 0))
        for h in range(2):
            over_mates(0, lambda i: to_pair(c, i, h).wait_send())
        over_mates(1, lambda other: across(c, 0, other).wait_send())
    over_mates(1, lambda other: across(g, 1, other).wait_send())
    for d in range(1, tps):
        sum_copy(lax.rem(my_tp + d, tps), my_tp).wait_send()
    store_ctx.wait()
    store_query.wait()


def body(n_ctx, tps, ctx_queries, ctx_keys, ctx_values, query_queries, query_keys, query_values, out_weight):
    block, heads_wide = ctx_queries.shape
    kv_wide = ctx_keys.shape[1]
    kv_local = kv_wide // HD
    group = heads_wide // kv_wide
    share = query_keys.shape[0]
    query_len = query_queries.shape[0]
    groups = kv_local
    members = n_ctx // groups
    flat = group * query_len
    chunk = flat // members
    pieces = math.gcd(members, block // 16)
    query_rows = -(-groups * share // 128) * 128
    out_cols = out_weight.shape[1]
    out_rows = query_len // tps
    dims = (groups, members, tps, kv_local, group, block, share, query_len)
    any_spec = pl.BlockSpec(memory_space=pltpu.HBM)
    dma = pltpu.SemaphoreType.DMA
    vmem = pltpu.VMEM
    return pl.pallas_call(
        functools.partial(kernel, dims),
        out_shape=(
            jax.ShapeDtypeStruct((block, heads_wide), BF16),
            jax.ShapeDtypeStruct((out_rows, out_cols), BF16),
        ),
        in_specs=[any_spec] * 7,
        out_specs=(any_spec, any_spec),
        scratch_shapes=[
            vmem((block, heads_wide), BF16),
            vmem((block, kv_wide), BF16),
            vmem((block, kv_wide), BF16),
            vmem((block, kv_wide), BF16),
            vmem((block, kv_wide), BF16),
            vmem((query_len, group * HD), BF16),
            vmem(out_weight.shape, BF16),
            vmem((groups, block, HD), BF16),
            vmem((groups, block, HD), BF16),
            vmem((query_rows, HD), BF16),
            vmem((query_rows, HD), BF16),
            vmem((flat, 2 * HD), F32),
            vmem((flat, HD), F32),
            vmem((members, chunk, HD), BF16),
            vmem((members, 8, chunk), F32),
            vmem((members, chunk, HD), BF16),
            vmem((members, 8, chunk), F32),
            vmem((query_len, heads_wide), BF16),
            vmem((tps, out_rows, out_cols), BF16),
            vmem((tps, out_rows, out_cols), BF16),
            vmem((block, heads_wide), BF16),
            vmem((out_rows, out_cols), BF16),
            vmem((block, block), F32),
            vmem((query_len, query_rows), F32),
            dma((13,)),
            dma((groups, 4)),
            dma((groups, 4)),
            dma((pieces, 2)),
            dma((2,)),
            dma((2,)),
            dma((members, 2)),
            dma((pieces, 2)),
            dma((members, 2)),
            dma((members, 2)),
            dma((groups, members, 2)),
            dma((groups, members, 2)),
            dma((groups, members, 2)),
            dma((groups, members, 2)),
            dma((groups, members, 2)),
            dma((tps,)),
            dma((tps,)),
        ],
        compiler_params=pltpu.CompilerParams(
            collective_id=0, has_side_effects=True, vmem_limit_bytes=64 * 1024 * 1024
        ),
        cost_estimate=pl.CostEstimate(flops=3_000_000_000, bytes_accessed=8_000_000, transcendentals=4_000_000),
        name="star_attention",
    )(ctx_queries, ctx_keys, ctx_values, query_queries, query_keys, query_values, out_weight)


def solution(mesh):
    return jax.shard_map(
        functools.partial(body, mesh.shape["ctx"], mesh.shape["tp"]),
        mesh=mesh,
        in_specs=(
            P("ctx", "tp"),
            P("ctx", "tp"),
            P("ctx", "tp"),
            P(None, "tp"),
            P("ctx", "tp"),
            P("ctx", "tp"),
            P("tp", "ctx"),
        ),
        out_specs=(P("ctx", "tp"), P("tp", "ctx")),
        check_vma=False,
    )
```

```python
import functools
import math

import jax
import jax.numpy as jnp
from jax import lax
from jax.experimental import pallas as pl
from jax.experimental.pallas import tpu as pltpu
from jax.sharding import PartitionSpec as P

HD = 128
MESH = pl.DeviceIdType.MESH
COEF = HD ** (-0.5) * math.log2(math.e)
F32 = jnp.float32
BF16 = jnp.bfloat16
NEG = float("-inf")


def kernel(dims, cq_h, ck_h, cv_h, qq_h, qk_h, qv_h, w_h, co_h, qo_h, cq, ck, cv, ak, av, qq, w, kb, vb, kqb, vqb,
           acc, top, osend, lsend, orecv, lrecv, att, ysend, yrecv, co, qo, own_bias, query_bias, loc_sem, kv_s, kv_r, an_s, an_r, an_u,
           an_rs, an_rr, rs_s, rs_r, ag_r, ag_u, ag_d, ag_rs, ag_cs, y_s, y_r):
    groups, members, tps, kv_local, group, block, share, query_len = dims
    flat = group * query_len
    chunk = flat // members
    tile = min(256, chunk)
    pieces = math.gcd(members, block // 16)
    piece = block // pieces
    me = lax.axis_index("ctx")
    my_tp = lax.axis_index("tp")
    g = lax.div(me, members)
    m = lax.rem(me, members)
    pair = m + 1 - 2 * lax.rem(m, 2)

    def lanes(index):
        return pl.ds(pl.multiple_of(index * HD, HD), HD)

    def local(src, dst, i):
        return pltpu.make_async_copy(src, dst, loc_sem.at[i])

    def remote(src, dst, send, recv, to, axis="ctx"):
        return pltpu.make_async_remote_copy(src_ref=src, dst_ref=dst, send_sem=send, recv_sem=recv,
                                            device_id={axis: to}, device_id_type=MESH)

    wide = pl.ds(pl.multiple_of(g * (group * HD), HD), group * HD)
    own_rows = pl.ds(pl.multiple_of(g * share, share), share)
    loads = [
        local(qq_h.at[:, wide], qq, 0),
        local(ck_h.at[:, lanes(g)], kb.at[g], 1),
        local(cv_h.at[:, lanes(g)], vb.at[g], 2),
        local(ck_h, ck, 3),
        local(cv_h, cv, 4),
        local(cq_h, cq, 5),
        local(w_h, w, 6),
        local(qk_h.at[:, lanes(g)], kqb.at[own_rows], 7),
        local(qv_h.at[:, lanes(g)], vqb.at[own_rows], 8),
    ]
    if kqb.shape[0] > groups * share:
        kqb[...] = jnp.zeros_like(kqb)
        vqb[...] = jnp.zeros_like(vqb)
    for load in loads:
        load.start()

    @pl.when(me == 0)
    def _():
        local(ck_h, ak, 9).start()
        local(cv_h, av, 10).start()

    barrier = pltpu.get_barrier_semaphore()

    def greet_group(i, carry):
        to = g * members + lax.rem(m + i, members)
        pl.semaphore_signal(barrier, inc=1, device_id={"ctx": to}, device_id_type=MESH)
        return carry

    lax.fori_loop(1, members, greet_group, 0)
    for d in range(1, groups):
        to = lax.rem(g + d, groups) * members + m
        pl.semaphore_signal(barrier, inc=1, device_id={"ctx": to}, device_id_type=MESH)
    for d in range(1, tps):
        pl.semaphore_signal(barrier, inc=1, device_id={"tp": lax.rem(my_tp + d, tps)}, device_id_type=MESH)
    pl.semaphore_wait(barrier, members - 1 + groups - 1 + tps - 1)

    def piece_rows(p):
        return pl.ds(pl.multiple_of(p * piece, piece), piece)

    @pl.when(me == 0)
    def _():
        local(ck_h, ak, 9).wait()
        local(cv_h, av, 10).wait()
        for p in range(1, pieces):
            for k, buf in enumerate((ak, av)):
                remote(buf.at[piece_rows(p)], buf.at[piece_rows(p)], an_s.at[p, k], an_r.at[k], p).start()

    def kv_copies(to_group, slot):
        to = to_group * members + m
        rows = pl.ds(pl.multiple_of(slot * share, share), share)
        return [
            remote(ck_h.at[:, lanes(to_group)], kb.at[slot], kv_s.at[to_group, 0], kv_r.at[slot, 0], to),
            remote(cv_h.at[:, lanes(to_group)], vb.at[slot], kv_s.at[to_group, 1], kv_r.at[slot, 1], to),
            remote(qk_h.at[:, lanes(to_group)], kqb.at[rows], kv_s.at[to_group, 2], kv_r.at[slot, 2], to),
            remote(qv_h.at[:, lanes(to_group)], vqb.at[rows], kv_s.at[to_group, 3], kv_r.at[slot, 3], to),
        ]

    def other_group(d):
        if groups & (groups - 1):
            return lax.rem(g + d, groups)
        other = g
        for bit in range(groups.bit_length()):
            if d >> bit & 1:
                other = other + (1 << bit) * (1 - 2 * lax.rem(lax.div(g, 1 << bit), 2))
        return other

    for d in range(1, groups):
        for copy in kv_copies(other_group(d), g)[2:]:
            copy.start()
    for d in range(1, groups):
        for copy in kv_copies(other_group(d), g)[:2]:
            copy.start()

    at = lax.broadcasted_iota(jnp.int32, own_bias.shape, 0)
    own_bias[...] = jnp.where(lax.broadcasted_iota(jnp.int32, own_bias.shape, 1) <= at, 0.0, NEG)
    col = lax.broadcasted_iota(jnp.int32, (1, query_bias.shape[1]), 1)
    position = (lax.div(col, share) * members + m) * share + lax.rem(col, share)
    position = jnp.where(col < groups * share, position, query_len)
    at = lax.broadcasted_iota(jnp.int32, query_bias.shape, 0)
    query_bias[...] = jnp.where(at >= position, 0.0, NEG)

    def attend(first_row, first, slot, with_query):
        head = lax.div(first_row, query_len)
        row = lax.rem(first_row, query_len)
        q = qq[pl.ds(pl.multiple_of(row, tile), tile), lanes(head)]
        keys, values = kb[slot], vb[slot]
        if with_query:
            keys = jnp.concatenate([keys, kqb[...]], 0)
            values = jnp.concatenate([values, vqb[...]], 0)
        values = jnp.concatenate([values, jnp.ones_like(values)], 1)
        s = lax.dot_general(q, keys, (((1,), (1,)), ((), ())), preferred_element_type=F32) * COEF
        if with_query:
            bias = query_bias[pl.ds(pl.multiple_of(row, tile), tile), :]
            s = jnp.concatenate([s[:, :block], s[:, block:] + bias], 1)
        rows = pl.ds(pl.multiple_of(first_row, tile), tile)
        high = jnp.max(s, axis=1, keepdims=True)
        if not first:
            before = top[rows, :]
            high = jnp.maximum(high, before[:, :1])
        p = jnp.exp2(s - high).astype(BF16)
        o = jnp.dot(p, values, preferred_element_type=F32)
        if not first:
            o = o + acc[rows, :] * jnp.exp2(before[:, :1] - high)
        acc[rows, :] = o
        top[rows, :] = jnp.broadcast_to(high, (tile, HD))

    def sweep(slot, first, with_query):
        def step(t, carry):
            attend(t * tile, first, slot, with_query)
            return carry

        lax.fori_loop(0, flat // tile, step, 0, unroll=2)

    for i in (0, 1, 2):
        loads[i].wait()
    if groups > 1:
        sweep(g, True, False)

    for i in (3, 4, 5, 6, 7, 8):
        loads[i].wait()
    not_root = me > 0
    has_piece = m < pieces

    @pl.when(has_piece)
    def _():
        mine = piece_rows(m)
        for k, buf in enumerate((ak, av)):
            @pl.when(not_root)
            def _():
                remote(buf.at[mine], buf.at[mine], an_u.at[k], an_r.at[k], me).wait_recv()

            @pl.when(g + 1 < groups)
            def _():
                remote(buf.at[mine], buf.at[mine], an_u.at[k], an_r.at[k], lax.rem(me + members, groups * members)).start()

        def spread(i, carry):
            other = lax.rem(m + i, members)

            @pl.when((g > 0) | (other > 0))
            def _():
                for k, buf in enumerate((ak, av)):
                    remote(buf.at[mine], buf.at[mine], an_rs.at[other, k], an_rr.at[m, k], g * members + other).start()
            return carry

        lax.fori_loop(1, members, spread, 0)

    anchor_bias = jnp.where(not_root, 0.0, NEG)

    def context_head(h):
        kv = lanes(lax.div(h, group))
        q = cq[:, lanes(h)]
        keys = jnp.concatenate([ak[:, kv], ck[:, kv]], 0)
        values = jnp.concatenate([av[:, kv], cv[:, kv]], 0)
        values = jnp.concatenate([values, jnp.ones_like(values)], 1)
        s = lax.dot_general(q, keys, (((1,), (1,)), ((), ())), preferred_element_type=F32) * COEF
        s = jnp.concatenate([s[:, :block] + anchor_bias, s[:, block:] + own_bias[...]], 1)
        p = jnp.exp2(s - jnp.max(s, axis=1, keepdims=True)).astype(BF16)
        o = jnp.dot(p, values, preferred_element_type=F32)
        co[:, lanes(h)] = (o[:, :HD] / o[:, HD:]).astype(BF16)

    heads = kv_local * group

    def context_heads(stage):
        first, end = stage * heads // groups, (stage + 1) * heads // groups

        def step(h, carry):
            context_head(h)
            return carry

        lax.fori_loop(first, end, step, 0, unroll=2)

    for d in range(1, groups):
        slot = other_group(d)
        if d == 1:
            for e in range(1, groups):
                for copy in kv_copies(other_group(e), other_group(e))[2:]:
                    copy.wait_recv()
        for copy in kv_copies(slot, slot)[:2]:
            copy.wait_recv()
        if d < groups - 1:
            sweep(slot, False, d == 1)
    last = other_group(groups - 1)

    def part(to):
        rows = pl.ds(pl.multiple_of(to * chunk, chunk), chunk)
        total = acc[rows, HD:]
        return acc[rows, :HD] / total, top[rows, :] + jnp.log2(total)

    def attend_chunk(to):
        for t in range(chunk // tile):
            attend(to * chunk + t * tile, groups == 1, last, groups <= 2)

    def part_copies(to, slot):
        target = g * members + to
        return [
            remote(osend.at[to], orecv.at[slot], rs_s.at[to, 0], rs_r.at[slot, 0], target),
            remote(lsend.at[to], lrecv.at[slot], rs_s.at[to, 1], rs_r.at[slot, 1], target),
        ]

    def send_part(i, carry):
        to = jnp.where(i < members - 1, lax.rem(m - lax.rem(m, 2) + 1 + i, members), pair)
        attend_chunk(to)
        out, lse = part(to)
        osend[to] = out.astype(BF16)
        lsend[to] = jnp.transpose(lse)[:8, :]
        for copy in part_copies(to, m):
            copy.start()
        return carry

    lax.fori_loop(1, members, send_part, 0)
    attend_chunk(m)

    @pl.when(not_root)
    def _():
        def gather(p, carry):
            @pl.when(p != m)
            def _():
                for k, buf in enumerate((ak, av)):
                    remote(buf.at[piece_rows(p)], buf.at[piece_rows(p)], an_u.at[k], an_rr.at[p, k], me).wait_recv()
            return carry

        lax.fori_loop(0, pieces, gather, 0)

    context_heads(0)

    def wait_part(i, carry):
        for copy in part_copies(lax.rem(m + i, members), lax.rem(m + i, members)):
            copy.wait_recv()
        return carry

    lax.fori_loop(1, members, wait_part, 0)

    def lse_of(i):
        row = lrecv[lax.rem(m + i, members)][:1, :]
        return jnp.transpose(jnp.broadcast_to(row, (HD, chunk)))

    own, own_lse = part(m)
    highest = lax.fori_loop(1, members, lambda i, high: jnp.maximum(high, lse_of(i)), own_lse)
    own_weight = jnp.exp2(own_lse - highest)

    def combine(i, carry):
        total, summed = carry
        weight = jnp.exp2(lse_of(i) - highest)
        return total + weight, summed + weight * orecv[lax.rem(m + i, members)].astype(F32)

    total, summed = lax.fori_loop(1, members, combine, (own_weight, own_weight * own))

    half = chunk // 2
    mates = members // 2

    def place(of_group, of_member, part_of):
        start = of_member * chunk
        row = pl.multiple_of(lax.rem(start, query_len) + part_of * half, half)
        return att.at[pl.ds(row, half), lanes(of_group * group + lax.div(start, query_len))]

    attended = (summed / total).astype(BF16)
    for h in range(2):
        place(g, m, h)[...] = attended[h * half:(h + 1) * half]

    def gathered(of_group, of_member, part_of, send, to):
        where = place(of_group, of_member, part_of)
        return remote(where, where, send, ag_r.at[of_group, of_member, part_of], to)

    def mate(i):
        return lax.rem(m + 2 * i, members)

    def over_mates(first, run):
        def step(i, carry):
            run(mate(i))
            return carry

        lax.fori_loop(first, mates, step, 0)

    up = lax.rem(me + members, groups * members)
    down = lax.rem(me + (groups - 1) * members, groups * members)

    def to_pair(c, i, h):
        return gathered(c, i, h, ag_cs.at[c, i, h], g * members + pair)

    def across(c, h, other):
        return gathered(c, m, h, ag_rs.at[c, other, h], g * members + other)

    def go_up(c, i, h):
        return gathered(c, i, h, ag_u.at[c, i, h], up)

    def go_down(c, i, h):
        return gathered(c, i, h, ag_d.at[c, i, h], down)

    def arrive(c, i, h):
        gathered(c, i, h, ag_cs.at[c, i, h], me).wait_recv()

    def relay_up(c, i, h):
        pl.when(g + 1 < groups)(lambda: go_up(c, i, h).start())

    def relay_down(c, i, h):
        pl.when(g > 0)(lambda: go_down(c, i, h).start())

    def when_low(s, run):
        pl.when(g - s >= 0)(lambda: run(jnp.maximum(g - s, 0)))

    def when_high(s, run):
        pl.when(g + s < groups)(lambda: run(jnp.minimum(g + s, groups - 1)))

    def from_column(relay):
        def run(c):
            arrive(c, m, 0)
            relay(c, m, 0)
            over_mates(1, lambda other: across(c, 0, other).start())
            to_pair(c, m, 0).start()

            def second(i):
                arrive(c, i, 1)
                relay(c, i, 1)
                to_pair(c, i, 1).start()

            over_mates(0, second)

        return run

    def from_row(c):
        def first_half(i):
            arrive(c, i, 0)
            to_pair(c, i, 0).start()

        over_mates(1, first_half)

    over_mates(1, lambda other: across(g, 1, other).start())
    for h in range(2):
        relay_up(g, m, h)
        relay_down(g, m, h)
    over_mates(1, lambda other: across(g, 0, other).start())
    for h in range(2):
        to_pair(g, m, h).start()

    def second_half(i):
        arrive(g, i, 1)
        relay_up(g, i, 1)
        relay_down(g, i, 1)
        to_pair(g, i, 1).start()

    over_mates(1, second_half)
    for s in range(1, groups):
        context_heads(s)
        when_low(s, from_column(relay_up))
        when_high(s, from_column(relay_down))
        if s == 1:
            from_row(g)
        else:
            when_low(s - 1, from_row)
            when_high(s - 1, from_row)
    if groups == 1:
        from_row(g)
    else:
        when_low(groups - 1, from_row)
        when_high(groups - 1, from_row)
    store_ctx = local(co, co_h, 11)
    store_ctx.start()

    def from_pair(i, carry):
        for c in range(groups):
            for h in range(2):
                arrive(c, lax.rem(pair + 2 * i, members), h)
        return carry

    lax.fori_loop(0, mates, from_pair, 0)

    out_rows = query_len // tps

    def project(of_tp):
        rows = pl.ds(pl.multiple_of(of_tp * out_rows, out_rows), out_rows)
        return jnp.dot(att[rows, :], w[...], preferred_element_type=F32)

    def sum_copy(of_tp, slot):
        return remote(ysend.at[of_tp], yrecv.at[slot], y_s.at[of_tp], y_r.at[slot], of_tp, "tp")

    for d in range(1, tps):
        to = lax.rem(my_tp + d, tps)
        ysend[to] = project(to).astype(BF16)
        sum_copy(to, my_tp).start()
    result = project(my_tp)
    for d in range(1, tps):
        source = lax.rem(my_tp + d, tps)
        sum_copy(source, source).wait_recv()
        result = result + yrecv[source].astype(F32)
    qo[...] = result.astype(BF16)
    store_query = local(qo, qo_h, 12)
    store_query.start()

    @pl.when(me == 0)
    def _():
        for p in range(1, pieces):
            for k, buf in enumerate((ak, av)):
                remote(buf.at[piece_rows(p)], buf.at[piece_rows(p)], an_s.at[p, k], an_r.at[k], p).wait_send()

    @pl.when(has_piece)
    def _():
        mine = piece_rows(m)

        @pl.when(g + 1 < groups)
        def _():
            for k, buf in enumerate((ak, av)):
                remote(buf.at[mine], buf.at[mine], an_u.at[k], an_r.at[k], me).wait_send()

        def spread_done(i, carry):
            other = lax.rem(m + i, members)

            @pl.when((g > 0) | (other > 0))
            def _():
                for k, buf in enumerate((ak, av)):
                    remote(buf.at[mine], buf.at[mine], an_rs.at[other, k], an_rr.at[m, k], me).wait_send()
            return carry

        lax.fori_loop(1, members, spread_done, 0)

    for d in range(1, groups):
        for copy in kv_copies(lax.rem(g + d, groups), g):
            copy.wait_send()

    def part_done(i, carry):
        for copy in part_copies(lax.rem(m + i, members), m):
            copy.wait_send()
        return carry

    lax.fori_loop(1, members, part_done, 0)

    def column_done(c, towards, can):
        @pl.when(can)
        def _():
            towards(c, m, 0).wait_send()
            over_mates(0, lambda i: towards(c, i, 1).wait_send())

    for c in range(groups):
        column_done(c, go_up, (c <= g) & (g + 1 < groups))
        column_done(c, go_down, (c >= g) & (g > 0))
        for h in range(2):
            over_mates(0, lambda i: to_pair(c, i, h).wait_send())
        over_mates(1, lambda other: across(c, 0, other).wait_send())
    over_mates(1, lambda other: across(g, 1, other).wait_send())
    for d in range(1, tps):
        sum_copy(lax.rem(my_tp + d, tps), my_tp).wait_send()
    store_ctx.wait()
    store_query.wait()


def body(n_ctx, tps, ctx_queries, ctx_keys, ctx_values, query_queries, query_keys, query_values, out_weight):
    block, heads_wide = ctx_queries.shape
    kv_wide = ctx_keys.shape[1]
    kv_local = kv_wide // HD
    group = heads_wide // kv_wide
    share = query_keys.shape[0]
    query_len = query_queries.shape[0]
    groups = kv_local
    members = n_ctx // groups
    flat = group * query_len
    chunk = flat // members
    pieces = math.gcd(members, block // 16)
    query_rows = -(-groups * share // 128) * 128
    out_cols = out_weight.shape[1]
    out_rows = query_len // tps
    dims = (groups, members, tps, kv_local, group, block, share, query_len)
    any_spec = pl.BlockSpec(memory_space=pltpu.HBM)
    dma = pltpu.SemaphoreType.DMA
    vmem = pltpu.VMEM
    return pl.pallas_call(
        functools.partial(kernel, dims),
        out_shape=(
            pltpu.VMEM((block, heads_wide), BF16),
            pltpu.VMEM((out_rows, out_cols), BF16),
        ),
        in_specs=[any_spec] * 7,
        out_specs=(pl.BlockSpec(memory_space=pl.ANY),) * 2,
        scratch_shapes=[
            vmem((block, heads_wide), BF16),
            vmem((block, kv_wide), BF16),
            vmem((block, kv_wide), BF16),
            vmem((block, kv_wide), BF16),
            vmem((block, kv_wide), BF16),
            vmem((query_len, group * HD), BF16),
            vmem(out_weight.shape, BF16),
            vmem((groups, block, HD), BF16),
            vmem((groups, block, HD), BF16),
            vmem((query_rows, HD), BF16),
            vmem((query_rows, HD), BF16),
            vmem((flat, 2 * HD), F32),
            vmem((flat, HD), F32),
            vmem((members, chunk, HD), BF16),
            vmem((members, 8, chunk), F32),
            vmem((members, chunk, HD), BF16),
            vmem((members, 8, chunk), F32),
            vmem((query_len, heads_wide), BF16),
            vmem((tps, out_rows, out_cols), BF16),
            vmem((tps, out_rows, out_cols), BF16),
            vmem((block, heads_wide), BF16),
            vmem((out_rows, out_cols), BF16),
            vmem((block, block), F32),
            vmem((query_len, query_rows), F32),
            dma((13,)),
            dma((groups, 4)),
            dma((groups, 4)),
            dma((pieces, 2)),
            dma((2,)),
            dma((2,)),
            dma((members, 2)),
            dma((pieces, 2)),
            dma((members, 2)),
            dma((members, 2)),
            dma((groups, members, 2)),
            dma((groups, members, 2)),
            dma((groups, members, 2)),
            dma((groups, members, 2)),
            dma((groups, members, 2)),
            dma((tps,)),
            dma((tps,)),
        ],
        compiler_params=pltpu.CompilerParams(
            collective_id=0, has_side_effects=True, vmem_limit_bytes=62 * 1024 * 1024
        ),
        cost_estimate=pl.CostEstimate(flops=3_000_000_000, bytes_accessed=8_000_000, transcendentals=4_000_000),
        name="star_attention",
    )(ctx_queries, ctx_keys, ctx_values, query_queries, query_keys, query_values, out_weight)


def solution(mesh):
    return jax.shard_map(
        functools.partial(body, mesh.shape["ctx"], mesh.shape["tp"]),
        mesh=mesh,
        in_specs=(
            P("ctx", "tp"),
            P("ctx", "tp"),
            P("ctx", "tp"),
            P(None, "tp"),
            P("ctx", "tp"),
            P("ctx", "tp"),
            P("tp", "ctx"),
        ),
        out_specs=(P("ctx", "tp"), P("tp", "ctx")),
        check_vma=False,
    )
```

```python
import functools
import math

import jax
import jax.numpy as jnp
from jax import lax
from jax.experimental import pallas as pl
from jax.experimental.pallas import tpu as pltpu
from jax.sharding import PartitionSpec as P

HD = 128
MESH = pl.DeviceIdType.MESH
COEF = HD ** (-0.5) * math.log2(math.e)
F32 = jnp.float32
BF16 = jnp.bfloat16
NEG = float("-inf")


def kernel(dims, cq_h, ck_h, cv_h, qq_h, qk_h, qv_h, w_h, co_h, qo_h, cq, ck, cv, ak, av, qq, w, kb, vb, kqb, vqb,
           acc, top, osend, lsend, orecv, lrecv, att, ysend, yrecv, co, qo, own_bias, query_bias, loc_sem, kv_s, kv_r, an_s, an_r, an_u,
           an_rs, an_rr, rs_s, rs_r, ag_r, ag_u, ag_d, ag_rs, ag_cs, y_s, y_r):
    groups, members, tps, kv_local, group, block, share, query_len = dims
    flat = group * query_len
    chunk = flat // members
    tile = min(256, chunk)
    pieces = math.gcd(members, block // 16)
    piece = block // pieces
    me = lax.axis_index("ctx")
    my_tp = lax.axis_index("tp")
    g = lax.div(me, members)
    m = lax.rem(me, members)
    pair = m + 1 - 2 * lax.rem(m, 2)

    def lanes(index):
        return pl.ds(pl.multiple_of(index * HD, HD), HD)

    def local(src, dst, i):
        return pltpu.make_async_copy(src, dst, loc_sem.at[i])

    def remote(src, dst, send, recv, to, axis="ctx"):
        return pltpu.make_async_remote_copy(src_ref=src, dst_ref=dst, send_sem=send, recv_sem=recv,
                                            device_id={axis: to}, device_id_type=MESH)

    wide = pl.ds(pl.multiple_of(g * (group * HD), HD), group * HD)
    own_rows = pl.ds(pl.multiple_of(g * share, share), share)
    loads = [
        local(qq_h.at[:, wide], qq, 0),
        local(ck_h.at[:, lanes(g)], kb.at[g], 1),
        local(cv_h.at[:, lanes(g)], vb.at[g], 2),
        local(ck_h, ck, 3),
        local(cv_h, cv, 4),
        local(cq_h, cq, 5),
        local(w_h, w, 6),
        local(qk_h.at[:, lanes(g)], kqb.at[own_rows], 7),
        local(qv_h.at[:, lanes(g)], vqb.at[own_rows], 8),
    ]
    if kqb.shape[0] > groups * share:
        kqb[...] = jnp.zeros_like(kqb)
        vqb[...] = jnp.zeros_like(vqb)
    for i in (3, 4, 0, 1, 2, 7, 8, 5, 6):
        loads[i].start()

    @pl.when(me == 0)
    def _():
        local(ck_h, ak, 9).start()
        local(cv_h, av, 10).start()

    barrier = pltpu.get_barrier_semaphore()

    def greet_group(i, carry):
        to = g * members + lax.rem(m + i, members)
        pl.semaphore_signal(barrier, inc=1, device_id={"ctx": to}, device_id_type=MESH)
        return carry

    lax.fori_loop(1, members, greet_group, 0)
    for d in range(1, groups):
        to = lax.rem(g + d, groups) * members + m
        pl.semaphore_signal(barrier, inc=1, device_id={"ctx": to}, device_id_type=MESH)
    for d in range(1, tps):
        pl.semaphore_signal(barrier, inc=1, device_id={"tp": lax.rem(my_tp + d, tps)}, device_id_type=MESH)
    pl.semaphore_wait(barrier, members - 1 + groups - 1 + tps - 1)

    def piece_rows(p):
        return pl.ds(pl.multiple_of(p * piece, piece), piece)

    @pl.when(me == 0)
    def _():
        local(ck_h, ak, 9).wait()
        local(cv_h, av, 10).wait()
        for p in range(1, pieces):
            for k, buf in enumerate((ak, av)):
                remote(buf.at[piece_rows(p)], buf.at[piece_rows(p)], an_s.at[p, k], an_r.at[k], p).start()

    loads[3].wait()
    loads[4].wait()

    def kv_copies(to_group, slot):
        to = to_group * members + m
        rows = pl.ds(pl.multiple_of(slot * share, share), share)
        return [
            remote(ck.at[:, lanes(to_group)], kb.at[slot], kv_s.at[to_group, 0], kv_r.at[slot, 0], to),
            remote(cv.at[:, lanes(to_group)], vb.at[slot], kv_s.at[to_group, 1], kv_r.at[slot, 1], to),
            remote(qk_h.at[:, lanes(to_group)], kqb.at[rows], kv_s.at[to_group, 2], kv_r.at[slot, 2], to),
            remote(qv_h.at[:, lanes(to_group)], vqb.at[rows], kv_s.at[to_group, 3], kv_r.at[slot, 3], to),
        ]

    def other_group(d):
        if groups & (groups - 1):
            return lax.rem(g + d, groups)
        other = g
        for bit in range(groups.bit_length()):
            if d >> bit & 1:
                other = other + (1 << bit) * (1 - 2 * lax.rem(lax.div(g, 1 << bit), 2))
        return other

    for d in range(1, groups):
        for copy in kv_copies(other_group(d), g)[2:]:
            copy.start()
    for d in range(1, groups):
        for copy in kv_copies(other_group(d), g)[:2]:
            copy.start()

    at = lax.broadcasted_iota(jnp.int32, own_bias.shape, 0)
    own_bias[...] = jnp.where(lax.broadcasted_iota(jnp.int32, own_bias.shape, 1) <= at, 0.0, NEG)
    col = lax.broadcasted_iota(jnp.int32, (1, query_bias.shape[1]), 1)
    position = (lax.div(col, share) * members + m) * share + lax.rem(col, share)
    position = jnp.where(col < groups * share, position, query_len)
    at = lax.broadcasted_iota(jnp.int32, query_bias.shape, 0)
    query_bias[...] = jnp.where(at >= position, 0.0, NEG)

    def attend(first_row, first, slot, with_query):
        head = lax.div(first_row, query_len)
        row = lax.rem(first_row, query_len)
        q = qq[pl.ds(pl.multiple_of(row, tile), tile), lanes(head)]
        keys, values = kb[slot], vb[slot]
        if with_query:
            keys = jnp.concatenate([keys, kqb[...]], 0)
            values = jnp.concatenate([values, vqb[...]], 0)
        values = jnp.concatenate([values, jnp.ones_like(values)], 1)
        s = lax.dot_general(q, keys, (((1,), (1,)), ((), ())), preferred_element_type=F32) * COEF
        if with_query:
            bias = query_bias[pl.ds(pl.multiple_of(row, tile), tile), :]
            s = jnp.concatenate([s[:, :block], s[:, block:] + bias], 1)
        rows = pl.ds(pl.multiple_of(first_row, tile), tile)
        high = jnp.max(s, axis=1, keepdims=True)
        if not first:
            before = top[rows, :]
            high = jnp.maximum(high, before[:, :1])
        p = jnp.exp2(s - high).astype(BF16)
        o = jnp.dot(p, values, preferred_element_type=F32)
        if not first:
            o = o + acc[rows, :] * jnp.exp2(before[:, :1] - high)
        acc[rows, :] = o
        top[rows, :] = jnp.broadcast_to(high, (tile, HD))

    def sweep(slot, first, with_query):
        def step(t, carry):
            attend(t * tile, first, slot, with_query)
            return carry

        lax.fori_loop(0, flat // tile, step, 0, unroll=2)

    for i in (0, 1, 2):
        loads[i].wait()
    if groups > 1:
        sweep(g, True, False)

    for i in (5, 6, 7, 8):
        loads[i].wait()
    not_root = me > 0
    has_piece = m < pieces

    @pl.when(has_piece)
    def _():
        mine = piece_rows(m)
        for k, buf in enumerate((ak, av)):
            @pl.when(not_root)
            def _():
                remote(buf.at[mine], buf.at[mine], an_u.at[k], an_r.at[k], me).wait_recv()

            @pl.when(g + 1 < groups)
            def _():
                remote(buf.at[mine], buf.at[mine], an_u.at[k], an_r.at[k], lax.rem(me + members, groups * members)).start()

        def spread(i, carry):
            other = lax.rem(m + i, members)

            @pl.when((g > 0) | (other > 0))
            def _():
                for k, buf in enumerate((ak, av)):
                    remote(buf.at[mine], buf.at[mine], an_rs.at[other, k], an_rr.at[m, k], g * members + other).start()
            return carry

        lax.fori_loop(1, members, spread, 0)

    anchor_bias = jnp.where(not_root, 0.0, NEG)

    def context_head(h):
        kv = lanes(lax.div(h, group))
        q = cq[:, lanes(h)]
        keys = jnp.concatenate([ak[:, kv], ck[:, kv]], 0)
        values = jnp.concatenate([av[:, kv], cv[:, kv]], 0)
        values = jnp.concatenate([values, jnp.ones_like(values)], 1)
        s = lax.dot_general(q, keys, (((1,), (1,)), ((), ())), preferred_element_type=F32) * COEF
        s = jnp.concatenate([s[:, :block] + anchor_bias, s[:, block:] + own_bias[...]], 1)
        p = jnp.exp2(s - jnp.max(s, axis=1, keepdims=True)).astype(BF16)
        o = jnp.dot(p, values, preferred_element_type=F32)
        co[:, lanes(h)] = (o[:, :HD] / o[:, HD:]).astype(BF16)

    heads = kv_local * group

    def context_heads(stage):
        first, end = stage * heads // groups, (stage + 1) * heads // groups

        def step(h, carry):
            context_head(h)
            return carry

        lax.fori_loop(first, end, step, 0, unroll=2)

    for d in range(1, groups):
        slot = other_group(d)
        if d == 1:
            for e in range(1, groups):
                for copy in kv_copies(other_group(e), other_group(e))[2:]:
                    copy.wait_recv()
        for copy in kv_copies(slot, slot)[:2]:
            copy.wait_recv()
        if d < groups - 1:
            sweep(slot, False, d == 1)
    last = other_group(groups - 1)

    def part(to):
        rows = pl.ds(pl.multiple_of(to * chunk, chunk), chunk)
        total = acc[rows, HD:]
        return acc[rows, :HD] / total, top[rows, :] + jnp.log2(total)

    def attend_chunk(to):
        for t in range(chunk // tile):
            attend(to * chunk + t * tile, groups == 1, last, groups <= 2)

    def part_copies(to, slot):
        target = g * members + to
        return [
            remote(osend.at[to], orecv.at[slot], rs_s.at[to, 0], rs_r.at[slot, 0], target),
            remote(lsend.at[to], lrecv.at[slot], rs_s.at[to, 1], rs_r.at[slot, 1], target),
        ]

    def send_part(i, carry):
        to = jnp.where(i < members - 1, lax.rem(m - lax.rem(m, 2) + 1 + i, members), pair)
        attend_chunk(to)
        out, lse = part(to)
        osend[to] = out.astype(BF16)
        lsend[to] = jnp.transpose(lse)[:8, :]
        for copy in part_copies(to, m):
            copy.start()
        return carry

    lax.fori_loop(1, members, send_part, 0)
    attend_chunk(m)

    @pl.when(not_root)
    def _():
        def gather(p, carry):
            @pl.when(p != m)
            def _():
                for k, buf in enumerate((ak, av)):
                    remote(buf.at[piece_rows(p)], buf.at[piece_rows(p)], an_u.at[k], an_rr.at[p, k], me).wait_recv()
            return carry

        lax.fori_loop(0, pieces, gather, 0)

    context_heads(0)

    def wait_part(i, carry):
        for copy in part_copies(lax.rem(m + i, members), lax.rem(m + i, members)):
            copy.wait_recv()
        return carry

    lax.fori_loop(1, members, wait_part, 0)

    def lse_of(i):
        row = lrecv[lax.rem(m + i, members)][:1, :]
        return jnp.transpose(jnp.broadcast_to(row, (HD, chunk)))

    own, own_lse = part(m)
    if members <= 8:
        lses = [own_lse] + [lse_of(i) for i in range(1, members)]
        highest = functools.reduce(jnp.maximum, lses)
        weights = [jnp.exp2(lse - highest) for lse in lses]
        total = sum(weights)
        summed = weights[0] * own
        for i in range(1, members):
            summed = summed + weights[i] * orecv[lax.rem(m + i, members)].astype(F32)
    else:
        highest = lax.fori_loop(1, members, lambda i, high: jnp.maximum(high, lse_of(i)), own_lse)
        own_weight = jnp.exp2(own_lse - highest)

        def combine(i, carry):
            total, summed = carry
            weight = jnp.exp2(lse_of(i) - highest)
            return total + weight, summed + weight * orecv[lax.rem(m + i, members)].astype(F32)

        total, summed = lax.fori_loop(1, members, combine, (own_weight, own_weight * own))

    half = chunk // 2
    mates = members // 2

    def place(of_group, of_member, part_of):
        start = of_member * chunk
        row = pl.multiple_of(lax.rem(start, query_len) + part_of * half, half)
        return att.at[pl.ds(row, half), lanes(of_group * group + lax.div(start, query_len))]

    attended = (summed / total).astype(BF16)
    for h in range(2):
        place(g, m, h)[...] = attended[h * half:(h + 1) * half]

    def gathered(of_group, of_member, part_of, send, to):
        where = place(of_group, of_member, part_of)
        return remote(where, where, send, ag_r.at[of_group, of_member, part_of], to)

    def mate(i):
        return lax.rem(m + 2 * i, members)

    def over_mates(first, run):
        def step(i, carry):
            run(mate(i))
            return carry

        lax.fori_loop(first, mates, step, 0)

    up = lax.rem(me + members, groups * members)
    down = lax.rem(me + (groups - 1) * members, groups * members)

    def to_pair(c, i, h):
        return gathered(c, i, h, ag_cs.at[c, i, h], g * members + pair)

    def across(c, h, other):
        return gathered(c, m, h, ag_rs.at[c, other, h], g * members + other)

    def go_up(c, i, h):
        return gathered(c, i, h, ag_u.at[c, i, h], up)

    def go_down(c, i, h):
        return gathered(c, i, h, ag_d.at[c, i, h], down)

    def arrive(c, i, h):
        gathered(c, i, h, ag_cs.at[c, i, h], me).wait_recv()

    def relay_up(c, i, h):
        pl.when(g + 1 < groups)(lambda: go_up(c, i, h).start())

    def relay_down(c, i, h):
        pl.when(g > 0)(lambda: go_down(c, i, h).start())

    def when_low(s, run):
        pl.when(g - s >= 0)(lambda: run(jnp.maximum(g - s, 0)))

    def when_high(s, run):
        pl.when(g + s < groups)(lambda: run(jnp.minimum(g + s, groups - 1)))

    def from_column(relay):
        def run(c):
            arrive(c, m, 0)
            relay(c, m, 0)
            over_mates(1, lambda other: across(c, 0, other).start())
            to_pair(c, m, 0).start()

            def second(i):
                arrive(c, i, 1)
                relay(c, i, 1)
                to_pair(c, i, 1).start()

            over_mates(0, second)

        return run

    def from_row(c):
        def first_half(i):
            arrive(c, i, 0)
            to_pair(c, i, 0).start()

        over_mates(1, first_half)

    over_mates(1, lambda other: across(g, 1, other).start())
    for h in range(2):
        relay_up(g, m, h)
        relay_down(g, m, h)
    over_mates(1, lambda other: across(g, 0, other).start())
    for h in range(2):
        to_pair(g, m, h).start()

    def second_half(i):
        arrive(g, i, 1)
        relay_up(g, i, 1)
        relay_down(g, i, 1)
        to_pair(g, i, 1).start()

    over_mates(1, second_half)
    for s in range(1, groups):
        context_heads(s)
        when_low(s, from_column(relay_up))
        when_high(s, from_column(relay_down))
        if s == 1:
            from_row(g)
        else:
            when_low(s - 1, from_row)
            when_high(s - 1, from_row)
    if groups == 1:
        from_row(g)
    else:
        when_low(groups - 1, from_row)
        when_high(groups - 1, from_row)
    store_ctx = local(co, co_h, 11)
    store_ctx.start()

    def from_pair(i, carry):
        for c in range(groups):
            for h in range(2):
                arrive(c, lax.rem(pair + 2 * i, members), h)
        return carry

    lax.fori_loop(0, mates, from_pair, 0)

    out_rows = query_len // tps

    def project(of_tp):
        rows = pl.ds(pl.multiple_of(of_tp * out_rows, out_rows), out_rows)
        return jnp.dot(att[rows, :], w[...], preferred_element_type=F32)

    def sum_copy(of_tp, slot):
        return remote(ysend.at[of_tp], yrecv.at[slot], y_s.at[of_tp], y_r.at[slot], of_tp, "tp")

    for d in range(1, tps):
        to = lax.rem(my_tp + d, tps)
        ysend[to] = project(to).astype(BF16)
        sum_copy(to, my_tp).start()
    result = project(my_tp)
    for d in range(1, tps):
        source = lax.rem(my_tp + d, tps)
        sum_copy(source, source).wait_recv()
        result = result + yrecv[source].astype(F32)
    qo[...] = result.astype(BF16)
    store_query = local(qo, qo_h, 12)
    store_query.start()

    @pl.when(me == 0)
    def _():
        for p in range(1, pieces):
            for k, buf in enumerate((ak, av)):
                remote(buf.at[piece_rows(p)], buf.at[piece_rows(p)], an_s.at[p, k], an_r.at[k], p).wait_send()

    @pl.when(has_piece)
    def _():
        mine = piece_rows(m)

        @pl.when(g + 1 < groups)
        def _():
            for k, buf in enumerate((ak, av)):
                remote(buf.at[mine], buf.at[mine], an_u.at[k], an_r.at[k], me).wait_send()

        def spread_done(i, carry):
            other = lax.rem(m + i, members)

            @pl.when((g > 0) | (other > 0))
            def _():
                for k, buf in enumerate((ak, av)):
                    remote(buf.at[mine], buf.at[mine], an_rs.at[other, k], an_rr.at[m, k], me).wait_send()
            return carry

        lax.fori_loop(1, members, spread_done, 0)

    for d in range(1, groups):
        for copy in kv_copies(lax.rem(g + d, groups), g):
            copy.wait_send()

    def part_done(i, carry):
        for copy in part_copies(lax.rem(m + i, members), m):
            copy.wait_send()
        return carry

    lax.fori_loop(1, members, part_done, 0)

    def column_done(c, towards, can):
        @pl.when(can)
        def _():
            towards(c, m, 0).wait_send()
            over_mates(0, lambda i: towards(c, i, 1).wait_send())

    for c in range(groups):
        column_done(c, go_up, (c <= g) & (g + 1 < groups))
        column_done(c, go_down, (c >= g) & (g > 0))
        for h in range(2):
            over_mates(0, lambda i: to_pair(c, i, h).wait_send())
        over_mates(1, lambda other: across(c, 0, other).wait_send())
    over_mates(1, lambda other: across(g, 1, other).wait_send())
    for d in range(1, tps):
        sum_copy(lax.rem(my_tp + d, tps), my_tp).wait_send()
    store_ctx.wait()
    store_query.wait()


def body(n_ctx, tps, ctx_queries, ctx_keys, ctx_values, query_queries, query_keys, query_values, out_weight):
    block, heads_wide = ctx_queries.shape
    kv_wide = ctx_keys.shape[1]
    kv_local = kv_wide // HD
    group = heads_wide // kv_wide
    share = query_keys.shape[0]
    query_len = query_queries.shape[0]
    groups = kv_local
    members = n_ctx // groups
    flat = group * query_len
    chunk = flat // members
    pieces = math.gcd(members, block // 16)
    query_rows = -(-groups * share // 128) * 128
    out_cols = out_weight.shape[1]
    out_rows = query_len // tps
    dims = (groups, members, tps, kv_local, group, block, share, query_len)
    any_spec = pl.BlockSpec(memory_space=pltpu.HBM)
    dma = pltpu.SemaphoreType.DMA
    vmem = pltpu.VMEM
    return pl.pallas_call(
        functools.partial(kernel, dims),
        out_shape=(
            pltpu.VMEM((block, heads_wide), BF16),
            pltpu.VMEM((out_rows, out_cols), BF16),
        ),
        in_specs=[any_spec] * 7,
        out_specs=(pl.BlockSpec(memory_space=pl.ANY),) * 2,
        scratch_shapes=[
            vmem((block, heads_wide), BF16),
            vmem((block, kv_wide), BF16),
            vmem((block, kv_wide), BF16),
            vmem((block, kv_wide), BF16),
            vmem((block, kv_wide), BF16),
            vmem((query_len, group * HD), BF16),
            vmem(out_weight.shape, BF16),
            vmem((groups, block, HD), BF16),
            vmem((groups, block, HD), BF16),
            vmem((query_rows, HD), BF16),
            vmem((query_rows, HD), BF16),
            vmem((flat, 2 * HD), F32),
            vmem((flat, HD), F32),
            vmem((members, chunk, HD), BF16),
            vmem((members, 8, chunk), F32),
            vmem((members, chunk, HD), BF16),
            vmem((members, 8, chunk), F32),
            vmem((query_len, heads_wide), BF16),
            vmem((tps, out_rows, out_cols), BF16),
            vmem((tps, out_rows, out_cols), BF16),
            vmem((block, heads_wide), BF16),
            vmem((out_rows, out_cols), BF16),
            vmem((block, block), F32),
            vmem((query_len, query_rows), F32),
            dma((13,)),
            dma((groups, 4)),
            dma((groups, 4)),
            dma((pieces, 2)),
            dma((2,)),
            dma((2,)),
            dma((members, 2)),
            dma((pieces, 2)),
            dma((members, 2)),
            dma((members, 2)),
            dma((groups, members, 2)),
            dma((groups, members, 2)),
            dma((groups, members, 2)),
            dma((groups, members, 2)),
            dma((groups, members, 2)),
            dma((tps,)),
            dma((tps,)),
        ],
        compiler_params=pltpu.CompilerParams(
            collective_id=0, has_side_effects=True, vmem_limit_bytes=62 * 1024 * 1024
        ),
        cost_estimate=pl.CostEstimate(flops=3_000_000_000, bytes_accessed=8_000_000, transcendentals=4_000_000),
        name="star_attention",
    )(ctx_queries, ctx_keys, ctx_values, query_queries, query_keys, query_values, out_weight)


def solution(mesh):
    return jax.shard_map(
        functools.partial(body, mesh.shape["ctx"], mesh.shape["tp"]),
        mesh=mesh,
        in_specs=(
            P("ctx", "tp"),
            P("ctx", "tp"),
            P("ctx", "tp"),
            P(None, "tp"),
            P("ctx", "tp"),
            P("ctx", "tp"),
            P("tp", "ctx"),
        ),
        out_specs=(P("ctx", "tp"), P("tp", "ctx")),
        check_vma=False,
    )
```

```python
import functools
import math

import jax
import jax.numpy as jnp
from jax import lax
from jax.experimental import pallas as pl
from jax.experimental.pallas import tpu as pltpu
from jax.sharding import PartitionSpec as P

HD = 128
MESH = pl.DeviceIdType.MESH
COEF = HD ** (-0.5) * math.log2(math.e)
F32 = jnp.float32
BF16 = jnp.bfloat16
NEG = float("-inf")


def kernel(dims, cq_h, ck_h, cv_h, qq_h, qk_h, qv_h, w_h, co_h, qo_h, cq, ck, cv, ak, av, qq, w, kb, vb, kqb, vqb,
           acc, top, osend, lsend, orecv, lrecv, att, ysend, yrecv, co, qo, own_bias, query_bias, loc_sem, kv_s, kv_r, an_s, an_r, an_u,
           an_rs, an_rr, rs_s, rs_r, ag_r, ag_u, ag_d, ag_rs, ag_cs, y_s, y_r):
    groups, members, tps, kv_local, group, block, share, query_len = dims
    flat = group * query_len
    chunk = flat // members
    tile = min(256, chunk)
    pieces = math.gcd(members, block // 16)
    piece = block // pieces
    me = lax.axis_index("ctx")
    my_tp = lax.axis_index("tp")
    g = lax.div(me, members)
    m = lax.rem(me, members)
    pair = m + 1 - 2 * lax.rem(m, 2)

    def lanes(index):
        return pl.ds(pl.multiple_of(index * HD, HD), HD)

    def local(src, dst, i):
        return pltpu.make_async_copy(src, dst, loc_sem.at[i])

    def remote(src, dst, send, recv, to, axis="ctx"):
        return pltpu.make_async_remote_copy(src_ref=src, dst_ref=dst, send_sem=send, recv_sem=recv,
                                            device_id={axis: to}, device_id_type=MESH)

    wide = pl.ds(pl.multiple_of(g * (group * HD), HD), group * HD)
    own_rows = pl.ds(pl.multiple_of(g * share, share), share)
    loads = [
        local(qq_h.at[:, wide], qq, 0),
        local(ck_h.at[:, lanes(g)], kb.at[g], 1),
        local(cv_h.at[:, lanes(g)], vb.at[g], 2),
        local(ck_h, ck, 3),
        local(cv_h, cv, 4),
        local(cq_h, cq, 5),
        local(w_h, w, 6),
        local(qk_h.at[:, lanes(g)], kqb.at[own_rows], 7),
        local(qv_h.at[:, lanes(g)], vqb.at[own_rows], 8),
    ]
    if kqb.shape[0] > groups * share:
        kqb[...] = jnp.zeros_like(kqb)
        vqb[...] = jnp.zeros_like(vqb)
    for i in (3, 4, 0, 1, 2, 7, 8, 5, 6):
        loads[i].start()

    @pl.when(me == 0)
    def _():
        local(ck_h, ak, 9).start()
        local(cv_h, av, 10).start()

    barrier = pltpu.get_barrier_semaphore()

    def greet_group(i, carry):
        to = g * members + lax.rem(m + i, members)
        pl.semaphore_signal(barrier, inc=1, device_id={"ctx": to}, device_id_type=MESH)
        return carry

    lax.fori_loop(1, members, greet_group, 0)
    for d in range(1, groups):
        to = lax.rem(g + d, groups) * members + m
        pl.semaphore_signal(barrier, inc=1, device_id={"ctx": to}, device_id_type=MESH)
    for d in range(1, tps):
        pl.semaphore_signal(barrier, inc=1, device_id={"tp": lax.rem(my_tp + d, tps)}, device_id_type=MESH)
    pl.semaphore_wait(barrier, members - 1 + groups - 1 + tps - 1)

    def piece_rows(p):
        return pl.ds(pl.multiple_of(p * piece, piece), piece)

    @pl.when(me == 0)
    def _():
        local(ck_h, ak, 9).wait()
        local(cv_h, av, 10).wait()
        for p in range(1, pieces):
            for k, buf in enumerate((ak, av)):
                remote(buf.at[piece_rows(p)], buf.at[piece_rows(p)], an_s.at[p, k], an_r.at[k], p).start()

    loads[3].wait()
    loads[4].wait()

    def kv_copies(to_group, slot):
        to = to_group * members + m
        rows = pl.ds(pl.multiple_of(slot * share, share), share)
        return [
            remote(ck.at[:, lanes(to_group)], kb.at[slot], kv_s.at[to_group, 0], kv_r.at[slot, 0], to),
            remote(cv.at[:, lanes(to_group)], vb.at[slot], kv_s.at[to_group, 1], kv_r.at[slot, 1], to),
            remote(qk_h.at[:, lanes(to_group)], kqb.at[rows], kv_s.at[to_group, 2], kv_r.at[slot, 2], to),
            remote(qv_h.at[:, lanes(to_group)], vqb.at[rows], kv_s.at[to_group, 3], kv_r.at[slot, 3], to),
        ]

    def other_group(d):
        if groups & (groups - 1):
            return lax.rem(g + d, groups)
        other = g
        for bit in range(groups.bit_length()):
            if d >> bit & 1:
                other = other + (1 << bit) * (1 - 2 * lax.rem(lax.div(g, 1 << bit), 2))
        return other

    for d in range(1, groups):
        for copy in kv_copies(other_group(d), g)[2:]:
            copy.start()
    for d in range(1, groups):
        for copy in kv_copies(other_group(d), g)[:2]:
            copy.start()

    at = lax.broadcasted_iota(jnp.int32, own_bias.shape, 0)
    own_bias[...] = jnp.where(lax.broadcasted_iota(jnp.int32, own_bias.shape, 1) <= at, 0.0, NEG)
    col = lax.broadcasted_iota(jnp.int32, (1, query_bias.shape[1]), 1)
    position = (lax.div(col, share) * members + m) * share + lax.rem(col, share)
    position = jnp.where(col < groups * share, position, query_len)
    at = lax.broadcasted_iota(jnp.int32, query_bias.shape, 0)
    query_bias[...] = jnp.where(at >= position, 0.0, NEG)

    def attend(first_row, first, slot, with_query):
        head = lax.div(first_row, query_len)
        row = lax.rem(first_row, query_len)
        q = qq[pl.ds(pl.multiple_of(row, tile), tile), lanes(head)]
        keys, values = kb[slot], vb[slot]
        if with_query:
            keys = jnp.concatenate([keys, kqb[...]], 0)
            values = jnp.concatenate([values, vqb[...]], 0)
        values = jnp.concatenate([values, jnp.ones_like(values)], 1)
        s = lax.dot_general(q, keys, (((1,), (1,)), ((), ())), preferred_element_type=F32) * COEF
        if with_query:
            bias = query_bias[pl.ds(pl.multiple_of(row, tile), tile), :]
            s = jnp.concatenate([s[:, :block], s[:, block:] + bias], 1)
        rows = pl.ds(pl.multiple_of(first_row, tile), tile)
        high = jnp.max(s, axis=1, keepdims=True)
        if not first:
            before = top[rows, :]
            high = jnp.maximum(high, before[:, :1])
        p = jnp.exp2(s - high).astype(BF16)
        o = jnp.dot(p, values, preferred_element_type=F32)
        if not first:
            o = o + acc[rows, :] * jnp.exp2(before[:, :1] - high)
        acc[rows, :] = o
        top[rows, :] = jnp.broadcast_to(high, (tile, HD))

    def sweep(slot, first, with_query):
        def step(t, carry):
            attend(t * tile, first, slot, with_query)
            return carry

        lax.fori_loop(0, flat // tile, step, 0, unroll=2)

    for i in (0, 1, 2):
        loads[i].wait()
    if groups > 1:
        sweep(g, True, False)

    for i in (5, 6, 7, 8):
        loads[i].wait()
    not_root = me > 0
    has_piece = m < pieces

    @pl.when(has_piece)
    def _():
        mine = piece_rows(m)
        for k, buf in enumerate((ak, av)):
            @pl.when(not_root)
            def _():
                remote(buf.at[mine], buf.at[mine], an_u.at[k], an_r.at[k], me).wait_recv()

            @pl.when(g + 1 < groups)
            def _():
                remote(buf.at[mine], buf.at[mine], an_u.at[k], an_r.at[k], lax.rem(me + members, groups * members)).start()

        def spread(i, carry):
            other = lax.rem(m + i, members)

            @pl.when((g > 0) | (other > 0))
            def _():
                for k, buf in enumerate((ak, av)):
                    remote(buf.at[mine], buf.at[mine], an_rs.at[other, k], an_rr.at[m, k], g * members + other).start()
            return carry

        lax.fori_loop(1, members, spread, 0)

    anchor_bias = jnp.where(not_root, 0.0, NEG)

    def context_head(h):
        kv = lanes(lax.div(h, group))
        q = cq[:, lanes(h)]
        keys = jnp.concatenate([ak[:, kv], ck[:, kv]], 0)
        values = jnp.concatenate([av[:, kv], cv[:, kv]], 0)
        values = jnp.concatenate([values, jnp.ones_like(values)], 1)
        s = lax.dot_general(q, keys, (((1,), (1,)), ((), ())), preferred_element_type=F32) * COEF
        s = jnp.concatenate([s[:, :block] + anchor_bias, s[:, block:] + own_bias[...]], 1)
        p = jnp.exp2(s - jnp.max(s, axis=1, keepdims=True)).astype(BF16)
        o = jnp.dot(p, values, preferred_element_type=F32)
        co[:, lanes(h)] = (o[:, :HD] / o[:, HD:]).astype(BF16)

    heads = kv_local * group

    def context_heads(stage):
        stages = max(groups - 1, 1)
        first, end = [min(i, stages) * heads // stages for i in (stage, stage + 1)]
        if first == end:
            return

        def step(h, carry):
            context_head(h)
            return carry

        lax.fori_loop(first, end, step, 0, unroll=2)

    for d in range(1, groups):
        slot = other_group(d)
        if d == 1:
            for e in range(1, groups):
                for copy in kv_copies(other_group(e), other_group(e))[2:]:
                    copy.wait_recv()
        for copy in kv_copies(slot, slot)[:2]:
            copy.wait_recv()
        if d < groups - 1:
            sweep(slot, False, d == 1)
    last = other_group(groups - 1)

    def part(to):
        rows = pl.ds(pl.multiple_of(to * chunk, chunk), chunk)
        total = acc[rows, HD:]
        return acc[rows, :HD] / total, top[rows, :] + jnp.log2(total)

    def attend_chunk(to):
        for t in range(chunk // tile):
            attend(to * chunk + t * tile, groups == 1, last, groups <= 2)

    def part_copies(to, slot):
        target = g * members + to
        return [
            remote(osend.at[to], orecv.at[slot], rs_s.at[to, 0], rs_r.at[slot, 0], target),
            remote(lsend.at[to], lrecv.at[slot], rs_s.at[to, 1], rs_r.at[slot, 1], target),
        ]

    def send_part(i, carry):
        to = jnp.where(i < members - 1, lax.rem(m - lax.rem(m, 2) + 1 + i, members), pair)
        attend_chunk(to)
        out, lse = part(to)
        osend[to] = out.astype(BF16)
        lsend[to] = jnp.transpose(lse)[:8, :]
        for copy in part_copies(to, m):
            copy.start()
        return carry

    lax.fori_loop(1, members, send_part, 0)
    attend_chunk(m)

    @pl.when(not_root)
    def _():
        def gather(p, carry):
            @pl.when(p != m)
            def _():
                for k, buf in enumerate((ak, av)):
                    remote(buf.at[piece_rows(p)], buf.at[piece_rows(p)], an_u.at[k], an_rr.at[p, k], me).wait_recv()
            return carry

        lax.fori_loop(0, pieces, gather, 0)

    context_heads(0)

    def wait_part(i, carry):
        for copy in part_copies(lax.rem(m + i, members), lax.rem(m + i, members)):
            copy.wait_recv()
        return carry

    lax.fori_loop(1, members, wait_part, 0)

    def lse_of(i):
        row = lrecv[lax.rem(m + i, members)][:1, :]
        return jnp.transpose(jnp.broadcast_to(row, (HD, chunk)))

    own, own_lse = part(m)
    if members <= 8:
        lses = [own_lse] + [lse_of(i) for i in range(1, members)]
        highest = functools.reduce(jnp.maximum, lses)
        weights = [jnp.exp2(lse - highest) for lse in lses]
        total = sum(weights)
        summed = weights[0] * own
        for i in range(1, members):
            summed = summed + weights[i] * orecv[lax.rem(m + i, members)].astype(F32)
    else:
        highest = lax.fori_loop(1, members, lambda i, high: jnp.maximum(high, lse_of(i)), own_lse)
        own_weight = jnp.exp2(own_lse - highest)

        def combine(i, carry):
            total, summed = carry
            weight = jnp.exp2(lse_of(i) - highest)
            return total + weight, summed + weight * orecv[lax.rem(m + i, members)].astype(F32)

        total, summed = lax.fori_loop(1, members, combine, (own_weight, own_weight * own))

    half = chunk // 2
    mates = members // 2

    def place(of_group, of_member, part_of):
        start = of_member * chunk
        row = pl.multiple_of(lax.rem(start, query_len) + part_of * half, half)
        return att.at[pl.ds(row, half), lanes(of_group * group + lax.div(start, query_len))]

    attended = (summed / total).astype(BF16)
    for h in range(2):
        place(g, m, h)[...] = attended[h * half:(h + 1) * half]

    def gathered(of_group, of_member, part_of, send, to):
        where = place(of_group, of_member, part_of)
        return remote(where, where, send, ag_r.at[of_group, of_member, part_of], to)

    def mate(i):
        return lax.rem(m + 2 * i, members)

    def over_mates(first, run):
        def step(i, carry):
            run(mate(i))
            return carry

        lax.fori_loop(first, mates, step, 0)

    up = lax.rem(me + members, groups * members)
    down = lax.rem(me + (groups - 1) * members, groups * members)

    def to_pair(c, i, h):
        return gathered(c, i, h, ag_cs.at[c, i, h], g * members + pair)

    def across(c, h, other):
        return gathered(c, m, h, ag_rs.at[c, other, h], g * members + other)

    def go_up(c, i, h):
        return gathered(c, i, h, ag_u.at[c, i, h], up)

    def go_down(c, i, h):
        return gathered(c, i, h, ag_d.at[c, i, h], down)

    def arrive(c, i, h):
        gathered(c, i, h, ag_cs.at[c, i, h], me).wait_recv()

    def relay_up(c, i, h):
        pl.when(g + 1 < groups)(lambda: go_up(c, i, h).start())

    def relay_down(c, i, h):
        pl.when(g > 0)(lambda: go_down(c, i, h).start())

    def when_low(s, run):
        pl.when(g - s >= 0)(lambda: run(jnp.maximum(g - s, 0)))

    def when_high(s, run):
        pl.when(g + s < groups)(lambda: run(jnp.minimum(g + s, groups - 1)))

    def from_column(relay):
        def run(c):
            arrive(c, m, 0)
            relay(c, m, 0)
            over_mates(1, lambda other: across(c, 0, other).start())
            to_pair(c, m, 0).start()

            def second(i):
                arrive(c, i, 1)
                relay(c, i, 1)
                to_pair(c, i, 1).start()

            over_mates(0, second)

        return run

    def from_row(c):
        def first_half(i):
            arrive(c, i, 0)
            to_pair(c, i, 0).start()

        over_mates(1, first_half)

    over_mates(1, lambda other: across(g, 1, other).start())
    for h in range(2):
        relay_up(g, m, h)
        relay_down(g, m, h)
    over_mates(1, lambda other: across(g, 0, other).start())
    for h in range(2):
        to_pair(g, m, h).start()

    def second_half(i):
        arrive(g, i, 1)
        relay_up(g, i, 1)
        relay_down(g, i, 1)
        to_pair(g, i, 1).start()

    over_mates(1, second_half)
    for s in range(1, groups):
        context_heads(s)
        when_low(s, from_column(relay_up))
        when_high(s, from_column(relay_down))
        if s == 1:
            from_row(g)
        else:
            when_low(s - 1, from_row)
            when_high(s - 1, from_row)
    if groups == 1:
        from_row(g)
    else:
        when_low(groups - 1, from_row)
        when_high(groups - 1, from_row)
    store_ctx = local(co, co_h, 11)
    store_ctx.start()

    def from_pair(i, carry):
        for c in range(groups):
            for h in range(2):
                arrive(c, lax.rem(pair + 2 * i, members), h)
        return carry

    lax.fori_loop(0, mates, from_pair, 0)

    out_rows = query_len // tps

    def project(of_tp):
        rows = pl.ds(pl.multiple_of(of_tp * out_rows, out_rows), out_rows)
        return jnp.dot(att[rows, :], w[...], preferred_element_type=F32)

    def sum_copy(of_tp, slot):
        return remote(ysend.at[of_tp], yrecv.at[slot], y_s.at[of_tp], y_r.at[slot], of_tp, "tp")

    for d in range(1, tps):
        to = lax.rem(my_tp + d, tps)
        ysend[to] = project(to).astype(BF16)
        sum_copy(to, my_tp).start()
    result = project(my_tp)
    for d in range(1, tps):
        source = lax.rem(my_tp + d, tps)
        sum_copy(source, source).wait_recv()
        result = result + yrecv[source].astype(F32)
    qo[...] = result.astype(BF16)
    store_query = local(qo, qo_h, 12)
    store_query.start()

    @pl.when(me == 0)
    def _():
        for p in range(1, pieces):
            for k, buf in enumerate((ak, av)):
                remote(buf.at[piece_rows(p)], buf.at[piece_rows(p)], an_s.at[p, k], an_r.at[k], p).wait_send()

    @pl.when(has_piece)
    def _():
        mine = piece_rows(m)

        @pl.when(g + 1 < groups)
        def _():
            for k, buf in enumerate((ak, av)):
                remote(buf.at[mine], buf.at[mine], an_u.at[k], an_r.at[k], me).wait_send()

        def spread_done(i, carry):
            other = lax.rem(m + i, members)

            @pl.when((g > 0) | (other > 0))
            def _():
                for k, buf in enumerate((ak, av)):
                    remote(buf.at[mine], buf.at[mine], an_rs.at[other, k], an_rr.at[m, k], me).wait_send()
            return carry

        lax.fori_loop(1, members, spread_done, 0)

    for d in range(1, groups):
        for copy in kv_copies(lax.rem(g + d, groups), g):
            copy.wait_send()

    def part_done(i, carry):
        for copy in part_copies(lax.rem(m + i, members), m):
            copy.wait_send()
        return carry

    lax.fori_loop(1, members, part_done, 0)

    def column_done(c, towards, can):
        @pl.when(can)
        def _():
            towards(c, m, 0).wait_send()
            over_mates(0, lambda i: towards(c, i, 1).wait_send())

    for c in range(groups):
        column_done(c, go_up, (c <= g) & (g + 1 < groups))
        column_done(c, go_down, (c >= g) & (g > 0))
        for h in range(2):
            over_mates(0, lambda i: to_pair(c, i, h).wait_send())
        over_mates(1, lambda other: across(c, 0, other).wait_send())
    over_mates(1, lambda other: across(g, 1, other).wait_send())
    for d in range(1, tps):
        sum_copy(lax.rem(my_tp + d, tps), my_tp).wait_send()
    store_ctx.wait()
    store_query.wait()


def body(n_ctx, tps, ctx_queries, ctx_keys, ctx_values, query_queries, query_keys, query_values, out_weight):
    block, heads_wide = ctx_queries.shape
    kv_wide = ctx_keys.shape[1]
    kv_local = kv_wide // HD
    group = heads_wide // kv_wide
    share = query_keys.shape[0]
    query_len = query_queries.shape[0]
    groups = kv_local
    members = n_ctx // groups
    flat = group * query_len
    chunk = flat // members
    pieces = math.gcd(members, block // 16)
    query_rows = -(-groups * share // 128) * 128
    out_cols = out_weight.shape[1]
    out_rows = query_len // tps
    dims = (groups, members, tps, kv_local, group, block, share, query_len)
    any_spec = pl.BlockSpec(memory_space=pltpu.HBM)
    dma = pltpu.SemaphoreType.DMA
    vmem = pltpu.VMEM
    return pl.pallas_call(
        functools.partial(kernel, dims),
        out_shape=(
            pltpu.VMEM((block, heads_wide), BF16),
            pltpu.VMEM((out_rows, out_cols), BF16),
        ),
        in_specs=[any_spec] * 7,
        out_specs=(pl.BlockSpec(memory_space=pl.ANY),) * 2,
        scratch_shapes=[
            vmem((block, heads_wide), BF16),
            vmem((block, kv_wide), BF16),
            vmem((block, kv_wide), BF16),
            vmem((block, kv_wide), BF16),
            vmem((block, kv_wide), BF16),
            vmem((query_len, group * HD), BF16),
            vmem(out_weight.shape, BF16),
            vmem((groups, block, HD), BF16),
            vmem((groups, block, HD), BF16),
            vmem((query_rows, HD), BF16),
            vmem((query_rows, HD), BF16),
            vmem((flat, 2 * HD), F32),
            vmem((flat, HD), F32),
            vmem((members, chunk, HD), BF16),
            vmem((members, 8, chunk), F32),
            vmem((members, chunk, HD), BF16),
            vmem((members, 8, chunk), F32),
            vmem((query_len, heads_wide), BF16),
            vmem((tps, out_rows, out_cols), BF16),
            vmem((tps, out_rows, out_cols), BF16),
            vmem((block, heads_wide), BF16),
            vmem((out_rows, out_cols), BF16),
            vmem((block, block), F32),
            vmem((query_len, query_rows), F32),
            dma((13,)),
            dma((groups, 4)),
            dma((groups, 4)),
            dma((pieces, 2)),
            dma((2,)),
            dma((2,)),
            dma((members, 2)),
            dma((pieces, 2)),
            dma((members, 2)),
            dma((members, 2)),
            dma((groups, members, 2)),
            dma((groups, members, 2)),
            dma((groups, members, 2)),
            dma((groups, members, 2)),
            dma((groups, members, 2)),
            dma((tps,)),
            dma((tps,)),
        ],
        compiler_params=pltpu.CompilerParams(
            collective_id=0, has_side_effects=True, vmem_limit_bytes=62 * 1024 * 1024
        ),
        cost_estimate=pl.CostEstimate(flops=3_000_000_000, bytes_accessed=8_000_000, transcendentals=4_000_000),
        name="star_attention",
    )(ctx_queries, ctx_keys, ctx_values, query_queries, query_keys, query_values, out_weight)


def solution(mesh):
    return jax.shard_map(
        functools.partial(body, mesh.shape["ctx"], mesh.shape["tp"]),
        mesh=mesh,
        in_specs=(
            P("ctx", "tp"),
            P("ctx", "tp"),
            P("ctx", "tp"),
            P(None, "tp"),
            P("ctx", "tp"),
            P("ctx", "tp"),
            P("tp", "ctx"),
        ),
        out_specs=(P("ctx", "tp"), P("tp", "ctx")),
        check_vma=False,
    )
```
